128 devices in a mesh: section: 16 (over y, z), tensor: 8 (over x, core).
Axes of the slice: x: 4, y: 4, z: 4, core: 2. Of those that a mesh axis runs over, the one named last changes fastest.
Arguments:
- hidden: bfloat16 [512, 8192], P('section', 'tensor'), may hold values from -16 to 16
- ref_hidden: bfloat16 [512, 8192], P('section', 'tensor'), may hold values from -16 to 16
- w_policy: bfloat16 [65536, 8192], P(('section', 'tensor')), may hold values from -0.5 to 0.5
- w_ref: bfloat16 [65536, 8192], P(('section', 'tensor')), may hold values from -0.5 to 0.5
- token_ids: int32 [512], replicated, may hold values from 0 to 65535
- loss_mask: int32 [512], replicated, may hold values 0 or 1
- advantages: float32 [512], replicated, may hold values from -4 to 4
Outputs:
- grad_hidden: float32 [512, 8192], P('section', 'tensor')
- grad_head: bfloat16 [65536, 8192], P(('section', 'tensor'))
The draws below stay inside these ranges and needn't reach their ends.
All inputs are finite; a program needn't handle non-finite values.
Results may differ from the reference program's by a relative error of at most 0.005.
Values may be sent and summed in bfloat16 or wider, within the bound.
A program may use at most 128 MiB of HBM per device.

```python
import math
import jax
import jax.numpy as jnp
import numpy as np
from jax import lax

D = 8192
TOKENS = 512
V = 65536
N_SECTION = 16


def draw_hidden(key, part):
    key = jax.random.fold_in(key, 1)
    values = jax.random.normal(key, (TOKENS, D), jnp.float32)
    return jnp.clip(values, -16.0, 16.0).astype(jnp.bfloat16)


def draw_ref_hidden(key, part):
    key = jax.random.fold_in(key, 2)
    values = jax.random.normal(key, (TOKENS, D), jnp.float32)
    return jnp.clip(values, -16.0, 16.0).astype(jnp.bfloat16)


def draw_w_policy(key, part):
    key = jax.random.fold_in(key, 3)
    values = jax.random.normal(key, (V, D), jnp.float32) * (3.0 / math.sqrt(D))
    return jnp.clip(values, -0.5, 0.5).astype(jnp.bfloat16)


def draw_w_ref(key, part):
    key = jax.random.fold_in(key, 4)
    values = jax.random.normal(key, (V, D), jnp.float32) * (3.0 / math.sqrt(D))
    return jnp.clip(values, -0.5, 0.5).astype(jnp.bfloat16)


def with_ends(drawn, own_key, least, top_value):
    dims = drawn.shape
    spot = [jax.random.randint(jax.random.fold_in(own_key, axis), (), 0, dims[axis]) for axis in range(len(dims))]
    drawn = drawn.at[tuple(spot)].set(least)
    longest = dims.index(max(dims))
    spot[longest] = (spot[longest] + 1) % dims[longest]
    return drawn.at[tuple(spot)].set(top_value)


def rank_bounds(count, skew):
    weights = [(1 << 20) // math.isqrt(standing ** skew) + 1 for standing in range(1, count + 1)]
    scale = 1 + sum(weights) // (1 << 30)
    return np.cumsum(np.array([max(1, weight // scale) for weight in weights]))


def skewed_ids(stream_key, shape, amount, lean):
    grid = rank_bounds(amount, lean)
    lot = jax.random.randint(jax.random.fold_in(stream_key, 1), shape, 0, int(grid[amount - 1]))
    rank = jnp.searchsorted(jnp.asarray(grid, jnp.int32), lot, side="right")
    return jax.random.permutation(jax.random.fold_in(stream_key, 2), amount)[rank].astype(jnp.int32)


def bell_draw(own_key, shape, deviation, bound, held_as=jnp.bfloat16):
    entries = jax.random.normal(own_key, shape, jnp.float32) * deviation
    return jnp.minimum(jnp.maximum(entries, -bound), bound).astype(held_as)


def setup_inputs(seed: int = 0) -> dict:
    seeds = jax.random.split(jax.random.key(seed), 8)
    return {
        "hidden": draw_hidden(jax.random.fold_in(seeds[7], 71), 0),
        "ref_hidden": draw_ref_hidden(jax.random.fold_in(seeds[7], 71), 0),
        "w_policy": draw_w_policy(jax.random.fold_in(seeds[7], 71), 0),
        "w_ref": draw_w_ref(jax.random.fold_in(seeds[7], 71), 0),
        "token_ids": with_ends(skewed_ids(seeds[4], (TOKENS,), V, 1), jax.random.fold_in(seeds[4], 3), 0, V - 1).astype(jnp.int32),
        "loss_mask": with_ends((jax.random.randint(seeds[5], (TOKENS,), 0, 4) < 3).astype(jnp.int32), jax.random.fold_in(seeds[5], 1), 0, 1),
        "advantages": bell_draw(seeds[6], (TOKENS,), 1.0, 4.0, jnp.float32),
    }


loss_scale = 4.0
penalty_weight = 0.2


def head_scores(rows_in, weights):
    return lax.dot_general(rows_in, weights, (((1,), (1,)), ((), ())), preferred_element_type=jnp.float32)


def normalized(scores):
    maximum = jnp.max(scores, axis=1, keepdims=True)
    return scores - (maximum + jnp.log(jnp.sum(jnp.exp(scores - maximum), axis=1, keepdims=True)))


def reference(hidden, ref_hidden, w_policy, w_ref, token_ids, loss_mask, advantages):
    logits = head_scores(hidden, w_policy)
    ref_logits = head_scores(ref_hidden, w_ref)
    log_probs = normalized(logits)
    ref_log_probs = normalized(ref_logits)
    probabilities = jnp.exp(log_probs)
    divergence = jnp.sum(probabilities * (log_probs - ref_log_probs), axis=1, keepdims=True)
    column = lax.broadcasted_iota(jnp.int32, logits.shape, 1)
    target = (column == token_ids.astype(jnp.int32)[:, None]).astype(jnp.float32)
    weight = loss_scale * loss_mask.astype(jnp.float32)[:, None]
    grad_logits = (weight * (advantages[:, None] * (probabilities - target) + penalty_weight * probabilities * (log_probs - ref_log_probs - divergence))).astype(jnp.bfloat16)
    grad_hidden = jnp.dot(grad_logits, w_policy, preferred_element_type=jnp.float32)
    blocks = grad_logits.T.reshape(N_SECTION, -1, grad_logits.shape[0])
    grad_head = lax.map(lambda vocab_block: jnp.dot(vocab_block, hidden, preferred_element_type=jnp.float32).astype(jnp.bfloat16), blocks).reshape(w_policy.shape)
    return grad_hidden, grad_head
```

```python
import functools

import jax
import jax.numpy as jnp
from jax import lax
from jax.experimental import pallas as pl
from jax.experimental.pallas import tpu as pltpu
from jax.sharding import PartitionSpec as P

MESH = pl.DeviceIdType.MESH
bf16, f32 = jnp.bfloat16, jnp.float32

loss_scale = 4.0
penalty_weight = 0.2

R = 16
H = 2
WIDTH = 1024
T = 16 * R
VW = 512
X, Y, Z = 0, 1, 2
ORDERS = ((X, Y, Z), (Y, Z, X), (Z, X, Y))
GATHER_COLS = (((0, 768), (768, 640), (1408, 640)), ((0, 640), (640, 640), (1280, 768)))
REDUCE_COLS = (((0, 384), (384, 384), (768, 256)), ((0, 384), (384, 256), (640, 384)))
ALL = slice(None)
LOW, HIGH = slice(0, 2), slice(2, 4)


def wrap(i):
    return lax.rem(i + 4, 4)


def pick(ref, lead, axes, where, cols):
    index = tuple(lead)
    for axis in axes:
        index += (where.get(axis, ALL),)
    return ref.at[index + (ALL, pl.ds(*cols))]


def kernel(
    hid, rhid, w_hbm, wr_hbm, tok, out_h, out_w,
    g, w, wr, lg, rlg, gv, gt, st_s, st_r,
    ysend, yrecv, s, fw, rl, rr, t3, fw2, rl2, rr2, t2, r1,
    load_sem, ag_send, ag_recv, dd_send, dd_recv, st_send, st_recv,
    y_send, y_recv, rs_send, rs_recv, out_sem,
):
    section, tensor = lax.axis_index("section"), lax.axis_index("tensor")
    x, c = tensor // 2, lax.rem(tensor, 2)
    y, z = section // 4, lax.rem(section, 4)
    me = (x, y, z)
    offset = (section * 8 + tensor) * VW

    def device(dx=0, dy=0, dz=0, dc=0):
        return (
            lax.rem(y + dy + 4, 4) * 4 + lax.rem(z + dz + 4, 4),
            lax.rem(x + dx + 4, 4) * 2 + lax.rem(c + dc, 2),
        )

    def along(axis, k):
        step = [0, 0, 0]
        step[axis] = k
        return device(*step)

    def send(src, dst, ssem, rsem, to):
        pltpu.make_async_remote_copy(
            src_ref=src, dst_ref=dst, send_sem=ssem, recv_sem=rsem, device_id=to, device_id_type=MESH
        ).start()

    def wait(ref, sem):
        pltpu.make_async_copy(ref, ref, sem).wait()

    tensor_peers = [(kx, kc) for kx in range(4) for kc in range(2) if (kx, kc) != (0, 0)]
    peers = [dict(dx=kx, dc=kc) for kx, kc in tensor_peers]
    peers += [dict(dy=k) for k in (1, 2, 3)] + [dict(dz=k) for k in (1, 2, 3)]

    loads = [
        pltpu.make_async_copy(
            src.at[pl.ds(h * R, R), :],
            g.at[h, c, x, y, z, :, pl.ds(m * WIDTH, WIDTH)],
            load_sem.at[2 * h + m],
        )
        for h in range(H)
        for m, src in enumerate((hid, rhid))
    ]
    for copy in loads:
        copy.start()
    weight_loads = [
        pltpu.make_async_copy(w_hbm, w, load_sem.at[4]),
        pltpu.make_async_copy(wr_hbm, wr, load_sem.at[5]),
    ]
    barrier = pltpu.get_barrier_semaphore()
    for peer in peers:
        pl.semaphore_signal(barrier, inc=1, device_id=device(**peer), device_id_type=MESH)
    for copy in loads:
        copy.wait()
    pl.semaphore_wait(barrier, len(peers))

    def ag_part(h, r, where):
        return pick(g, (h, c), (X, Y, Z), where, GATHER_COLS[h][r])

    def ag_send_part(h, r, where, axis, k, event):
        part = ag_part(h, r, where)
        send(part, part, ag_send.at[h], ag_recv.at[h, r, event], along(axis, k))

    def ag_core(h, r, where):
        part = ag_part(h, r, where)
        send(part, part, dd_send.at[h], dd_recv.at[h], device(dc=1))

    def ag_wait(h, r, event, where):
        wait(ag_part(h, r, where), ag_recv.at[h, r, event])

    one_line, two_lines, four_lines = {X: 0, Y: 0}, {X: 0, Y: slice(0, 2)}, {X: 0}

    def ag0(h):
        for r, (a1, a2, a3) in enumerate(ORDERS):
            for k in (1, 3, 2):
                ag_send_part(h, r, {a1: me[a1], a2: me[a2], a3: me[a3]}, a1, k, 0)

    def ag1(h):
        for r, (a1, a2, a3) in enumerate(ORDERS):
            ag_wait(h, r, 0, {X: 0, Y: 0, Z: slice(0, 3)})
            line = {a2: me[a2], a3: me[a3]}
            for k in (1, 3):
                ag_send_part(h, r, line, a2, k, 1)
            for k in (1, 3):
                ag_send_part(h, r, line, a3, k, 3)
            ag_core(h, r, line)

    def ag2(h):
        for r, (a1, a2, a3) in enumerate(ORDERS):
            m2, m3 = me[a2], me[a3]
            ag_wait(h, r, 1, two_lines)
            left, right = wrap(m2 - 1), wrap(m2 + 1)
            ag_send_part(h, r, {a1: LOW, a2: left, a3: m3}, a2, 1, 2)
            ag_send_part(h, r, {a1: HIGH, a2: right, a3: m3}, a2, 3, 2)
            for j in (left, right):
                for k in (1, 3):
                    ag_send_part(h, r, {a2: j, a3: m3}, a3, k, 4)
                ag_core(h, r, {a2: j, a3: m3})

    def ag_last(h, r, lines, event, waited):
        a1, a2, a3 = ORDERS[r]
        left, right = wrap(me[a3] - 1), wrap(me[a3] + 1)
        ag_wait(h, r, event, waited)
        for j in lines:
            ag_send_part(h, r, {a1: LOW, a2: j, a3: left}, a3, 1, 6)
            ag_send_part(h, r, {a1: HIGH, a2: j, a3: right}, a3, 3, 6)
        for j in lines:
            ag_core(h, r, {a2: j, a3: left})
            ag_core(h, r, {a2: j, a3: right})

    def ag3(h):
        for r, (a1, a2, a3) in enumerate(ORDERS):
            ag_last(h, r, (me[a2],), 3, two_lines)

    def ag4(h):
        for r, (a1, a2, a3) in enumerate(ORDERS):
            ag_wait(h, r, 2, one_line)
            line = {a2: wrap(me[a2] + 2), a3: me[a3]}
            for k in (1, 3):
                ag_send_part(h, r, line, a3, k, 5)
            ag_core(h, r, line)

    def ag5(h):
        for r, (a1, a2, a3) in enumerate(ORDERS):
            ag_last(h, r, (wrap(me[a2] - 1), wrap(me[a2] + 1)), 4, four_lines)

    def ag6(h):
        for r, (a1, a2, a3) in enumerate(ORDERS):
            ag_last(h, r, (wrap(me[a2] + 2),), 5, two_lines)

    def ag7(h):
        for r, (a1, a2, a3) in enumerate(ORDERS):
            ag_wait(h, r, 6, four_lines)
            ag_core(h, r, {a3: wrap(me[a3] + 2)})

    def ag_core_wait(h):
        wait(g.at[h, 1 - c], dd_recv.at[h])

    def logits(h, core, first, last):
        def step(i, carry):
            column = pl.multiple_of((i * 2 + core) * WIDTH, WIDTH)
            for m, (weights, acc) in enumerate(((w, lg), (wr, rlg))):
                rows = g[h, core, i, :, :, :, m * WIDTH:(m + 1) * WIDTH].reshape(T, WIDTH)
                acc[h] += lax.dot_general(
                    weights[:, pl.ds(column, WIDTH)], rows, (((1,), (1,)), ((), ())), preferred_element_type=f32
                )
            return carry

        lax.fori_loop(first, last, step, 0)

    def clear(h):
        lg[h] = jnp.zeros((VW, T), f32)
        rlg[h] = jnp.zeros((VW, T), f32)

    def local_stats(h):
        l, rf = lg[h], rlg[h]
        m = jnp.max(l, axis=0, keepdims=True)
        rm = jnp.max(rf, axis=0, keepdims=True)
        lm, rfm = l - m, rf - rm
        e = jnp.exp(lm)
        mass = jnp.sum(e, axis=0, keepdims=True)
        rmass = jnp.sum(jnp.exp(rfm), axis=0, keepdims=True)
        d = jnp.sum(e * (lm - rfm), axis=0, keepdims=True)
        st_s[h, 0] = jnp.concatenate([m, mass, rm, rmass, d, d, d, d], axis=0)

    groups = (
        [dict(dx=kx, dc=kc) for kx, kc in tensor_peers],
        [dict(dy=k) for k in (1, 2, 3)],
        [dict(dz=k) for k in (1, 2, 3)],
    )
    starts = (0, 7, 10)

    def stats_send(h, phase):
        for i, peer in enumerate(groups[phase]):
            send(
                st_s.at[h, phase], st_r.at[h, starts[phase] + i],
                st_send.at[h, phase], st_recv.at[h, phase], device(**peer),
            )

    def stats_wait(h, phase):
        n = len(groups[phase])
        wait(st_r.at[h, pl.ds(starts[phase], n)], st_recv.at[h, phase])
        terms = [st_s[h, phase]] + [st_r[h, starts[phase] + i] for i in range(n)]
        m = functools.reduce(jnp.maximum, [a[0:1] for a in terms])
        rm = functools.reduce(jnp.maximum, [a[2:3] for a in terms])
        mass, rmass, d = 0.0, 0.0, 0.0
        for a in terms:
            dm, drm = a[0:1] - m, a[2:3] - rm
            scale = jnp.exp(dm)
            mass += scale * a[1:2]
            rmass += jnp.exp(drm) * a[3:4]
            d += scale * (a[4:5] + a[1:2] * (dm - drm))
        st_s[h, phase + 1] = jnp.concatenate([m, mass, rm, rmass, d, d, d, d], axis=0)

    def grads(h):
        a = st_s[h, 3]
        m, mass, rm, rmass, d = a[0:1], a[1:2], a[2:3], a[3:4], a[4:5]
        ln, rln = jnp.log(mass), jnp.log(rmass)
        divergence = d / mass - ln + rln
        ids, mask, adv = tok[h, 0:1], tok[h, 1:2], tok[h, 2:3]
        weight = loss_scale * mask
        place = ids - offset.astype(f32)

        def step(i, carry):
            rows = pl.multiple_of(i * 128, 128)
            lp = (lg[h, pl.ds(rows, 128), :] - m) - ln
            rlp = (rlg[h, pl.ds(rows, 128), :] - rm) - rln
            p = jnp.exp(lp)
            entry = (rows + lax.broadcasted_iota(jnp.int32, (128, T), 0)).astype(f32)
            target = (entry == place).astype(f32)
            value = weight * (adv * (p - target) + penalty_weight * p * (lp - rlp - divergence))
            gv[pl.ds(rows, 128), h * T:(h + 1) * T] = value.astype(bf16)
            gt[h, :, pl.ds(rows, 128)] = value.T.astype(bf16)
            return carry

        lax.fori_loop(0, VW // 128, step, 0)

    def products_other(h):
        for i in range(4):
            column = pl.multiple_of((i * 2 + 1 - c) * WIDTH, WIDTH)
            rows = jnp.dot(gt[h], w[:, pl.ds(column, WIDTH)], preferred_element_type=f32)
            ysend[h, i] = rows.astype(bf16).reshape(4, 4, R, WIDTH)
            send(ysend.at[h, i], yrecv.at[h, i], y_send.at[h], y_recv.at[h, i], device(dc=1))

    def products_own(h):
        for i in range(4):
            column = pl.multiple_of((i * 2 + c) * WIDTH, WIDTH)
            rows = jnp.dot(gt[h], w[:, pl.ds(column, WIDTH)], preferred_element_type=f32)
            wait(yrecv.at[h, i], y_recv.at[h, i])
            rows += yrecv[h, i].reshape(T, WIDTH).astype(f32)
            s[h, i] = rows.astype(bf16).reshape(4, 4, R, WIDTH)

    def rs_axes(r):
        a1, a2, a3 = ORDERS[r]
        plane = tuple(a for a in (X, Y, Z) if a != a3)
        return a1, a2, a3, plane

    def rs3_start(h):
        for r in range(3):
            a1, a2, a3, plane = rs_axes(r)
            m3, cols = me[a3], REDUCE_COLS[h][r]
            at = lambda ref, where: pick(ref, (h,), plane, where, cols)
            mine = lambda where: pick(s, (h,), (X, Y, Z), where, cols)
            right, left, far = wrap(m3 + 1), wrap(m3 - 1), wrap(m3 + 2)
            ss = rs_send.at[h, 0]
            send(mine({a1: LOW, a3: far}), at(fw, {a1: LOW}), ss, rs_recv.at[h, r, 0], along(a3, 1))
            send(mine({a1: HIGH, a3: far}), at(fw, {a1: HIGH}), ss, rs_recv.at[h, r, 0], along(a3, 3))
        for r in range(3):
            a1, a2, a3, plane = rs_axes(r)
            m3, cols = me[a3], REDUCE_COLS[h][r]
            at = lambda ref, where: pick(ref, (h,), plane, where, cols)
            mine = lambda where: pick(s, (h,), (X, Y, Z), where, cols)
            right, left = wrap(m3 + 1), wrap(m3 - 1)
            ss = rs_send.at[h, 0]
            send(mine({a1: HIGH, a3: right}), at(rl, {a1: HIGH}), ss, rs_recv.at[h, r, 1], along(a3, 1))
            send(mine({a1: LOW, a3: left}), at(rr, {a1: LOW}), ss, rs_recv.at[h, r, 1], along(a3, 3))

    def rs3_middle(h):
        for r in range(3):
            a1, a2, a3, plane = rs_axes(r)
            m3, cols = me[a3], REDUCE_COLS[h][r]
            at = lambda ref, where: pick(ref, (h,), plane, where, cols)
            mine = lambda where: pick(s, (h,), (X, Y, Z), where, cols)
            wait(at(fw, {}), rs_recv.at[h, r, 0])
            for part, to, k, dst in ((LOW, wrap(m3 + 1), 1, rl), (HIGH, wrap(m3 - 1), 3, rr)):
                place = at(fw, {a1: part})
                place[...] = (place[...].astype(f32) + mine({a1: part, a3: to})[...].astype(f32)).astype(bf16)
                send(place, at(dst, {a1: part}), rs_send.at[h, 0], rs_recv.at[h, r, 2], along(a3, k))

    def rs3_end(h):
        for r in range(3):
            a1, a2, a3, plane = rs_axes(r)
            m3, m2, cols = me[a3], me[a2], REDUCE_COLS[h][r]
            at = lambda ref, where: pick(ref, (h,), plane, where, cols)
            mine = lambda where: pick(s, (h,), (X, Y, Z), where, cols)
            line = lambda ref, where: pick(ref, (h,), (a1,), where, cols)
            wait(at(rl, {}), rs_recv.at[h, r, 1])
            wait(at(rr, {}), rs_recv.at[h, r, 2])
            total = mine({a3: m3})[...].astype(f32) + at(rl, {})[...].astype(f32) + at(rr, {})[...].astype(f32)
            at(t3, {})[...] = total.astype(bf16)
            far, right, left = wrap(m2 + 2), wrap(m2 + 1), wrap(m2 - 1)
            ss = rs_send.at[h, 1]
            send(at(t3, {a1: LOW, a2: far}), line(fw2, {a1: LOW}), ss, rs_recv.at[h, r, 3], along(a2, 1))
            send(at(t3, {a1: HIGH, a2: far}), line(fw2, {a1: HIGH}), ss, rs_recv.at[h, r, 3], along(a2, 3))
            send(at(t3, {a1: HIGH, a2: right}), line(rl2, {a1: HIGH}), ss, rs_recv.at[h, r, 4], along(a2, 1))
            send(at(t3, {a1: LOW, a2: left}), line(rr2, {a1: LOW}), ss, rs_recv.at[h, r, 4], along(a2, 3))

    def rs2_middle(h):
        for r in range(3):
            a1, a2, a3, plane = rs_axes(r)
            m2, cols = me[a2], REDUCE_COLS[h][r]
            at = lambda ref, where: pick(ref, (h,), plane, where, cols)
            line = lambda ref, where: pick(ref, (h,), (a1,), where, cols)
            wait(line(fw2, {}), rs_recv.at[h, r, 3])
            for part, to, k, dst in ((LOW, wrap(m2 + 1), 1, rl2), (HIGH, wrap(m2 - 1), 3, rr2)):
                place = line(fw2, {a1: part})
                place[...] = (place[...].astype(f32) + at(t3, {a1: part, a2: to})[...].astype(f32)).astype(bf16)
                send(place, line(dst, {a1: part}), rs_send.at[h, 1], rs_recv.at[h, r, 5], along(a2, k))

    def rs2_end(h):
        for r in range(3):
            a1, a2, a3, plane = rs_axes(r)
            m1, m2, cols = me[a1], me[a2], REDUCE_COLS[h][r]
            at = lambda ref, where: pick(ref, (h,), plane, where, cols)
            line = lambda ref, where: pick(ref, (h,), (a1,), where, cols)
            wait(line(rl2, {}), rs_recv.at[h, r, 4])
            wait(line(rr2, {}), rs_recv.at[h, r, 5])
            total = at(t3, {a2: m2})[...].astype(f32) + line(rl2, {})[...].astype(f32)
            line(t2, {})[...] = total + line(rr2, {})[...].astype(f32)
            for k in (1, 2, 3):
                send(
                    line(t2, {a1: wrap(m1 + k)}), pick(r1, (h,), (a1,), {a1: k - 1}, cols),
                    rs_send.at[h, 2], rs_recv.at[h, r, 6], along(a1, k),
                )

    def rs1_end(h):
        for r in range(3):
            a1, a2, a3, plane = rs_axes(r)
            cols = REDUCE_COLS[h][r]
            wait(pick(r1, (h,), (a1,), {}, cols), rs_recv.at[h, r, 6])
            total = pick(t2, (h,), (a1,), {a1: me[a1]}, cols)[...]
            for k in range(3):
                total += pick(r1, (h,), (a1,), {a1: k}, cols)[...]
            out_h[h * R:(h + 1) * R, cols[0]:cols[0] + cols[1]] = total

    def head(first, last):
        def step(i, carry):
            core, col = lax.rem(i, 2), i // 2
            column = pl.multiple_of(i * WIDTH, WIDTH)
            total = 0.0
            for h in range(H):
                rows = g[h, core, col, :, :, :, 0:WIDTH].reshape(T, WIDTH)
                total += jnp.dot(gv[:, h * T:(h + 1) * T], rows, preferred_element_type=f32)
            wr[:, pl.ds(column, WIDTH)] = total.astype(bf16)
            pltpu.make_async_copy(
                wr.at[:, pl.ds(column, WIDTH)], out_w.at[:, pl.ds(column, WIDTH)], out_sem
            ).start()
            return carry

        lax.fori_loop(first, last, step, 0)

    ag0(0)
    for copy in weight_loads:
        copy.start()
    clear(0)
    clear(1)
    ag1(0)
    ag0(1)
    ag2(0)
    ag3(0)
    ag1(1)
    ag4(0)
    ag5(0)
    ag2(1)
    ag6(0)
    ag3(1)
    ag7(0)
    for copy in weight_loads:
        copy.wait()
    logits(0, c, 0, 2)
    ag4(1)
    logits(0, c, 2, 4)
    ag5(1)
    ag_core_wait(0)
    logits(0, 1 - c, 0, 4)
    ag6(1)
    local_stats(0)
    stats_send(0, 0)
    stats_wait(0, 0)
    stats_send(0, 1)
    stats_wait(0, 1)
    stats_send(0, 2)
    ag7(1)
    stats_wait(0, 2)
    grads(0)
    products_other(0)
    products_own(0)
    rs3_start(0)
    logits(1, c, 0, 4)
    ag_core_wait(1)
    logits(1, 1 - c, 0, 2)
    rs3_middle(0)
    logits(1, 1 - c, 2, 4)
    local_stats(1)
    stats_send(1, 0)
    stats_wait(1, 0)
    stats_send(1, 1)
    rs3_end(0)
    stats_wait(1, 1)
    stats_send(1, 2)
    rs2_middle(0)
    stats_wait(1, 2)
    grads(1)
    products_other(1)
    products_own(1)
    rs3_start(1)
    rs2_end(0)
    head(0, 4)
    rs3_middle(1)
    rs1_end(0)
    head(4, 8)
    rs3_end(1)
    rs2_middle(1)
    rs2_end(1)
    rs1_end(1)

    wait(wr, out_sem)
    for h in range(H):
        wait(w.at[pl.ds(0, 256), pl.ds(0, 63 * 128)], ag_send.at[h])
        wait(g.at[h, c], dd_send.at[h])
        for phase in range(3):
            n = len(groups[phase])
            wait(st_r.at[h, pl.ds(starts[phase], n)], st_send.at[h, phase])
        wait(ysend.at[h], y_send.at[h])
        wait(s.at[h, pl.ds(0, 3)], rs_send.at[h, 0])
        wait(s.at[h, 0, pl.ds(0, 3)], rs_send.at[h, 1])
        wait(t2.at[h, pl.ds(0, 3)], rs_send.at[h, 2])


def shards(hidden, ref_hidden, w_policy, w_ref, token_ids, loss_mask, advantages):
    by_half = lambda a: a.astype(f32).reshape(16, H, R).transpose(1, 0, 2).reshape(H, 1, T)
    tok = jnp.concatenate([by_half(token_ids), by_half(loss_mask), by_half(advantages)], axis=1)
    tok = jnp.pad(tok, ((0, 0), (0, 5), (0, 0)))
    any_space = pl.BlockSpec(memory_space=pl.ANY)
    vmem = pl.BlockSpec(memory_space=pltpu.VMEM)
    dma = pltpu.SemaphoreType.DMA
    return pl.pallas_call(
        kernel,
        out_shape=(
            jax.ShapeDtypeStruct((H * R, WIDTH), f32),
            jax.ShapeDtypeStruct((VW, 8 * WIDTH), bf16),
        ),
        in_specs=[any_space] * 4 + [vmem],
        out_specs=(vmem, any_space),
        scratch_shapes=[
            pltpu.VMEM((H, 2, 4, 4, 4, R, 2 * WIDTH), bf16),
            pltpu.VMEM((VW, 8 * WIDTH), bf16),
            pltpu.VMEM((VW, 8 * WIDTH), bf16),
            pltpu.VMEM((H, VW, T), f32),
            pltpu.VMEM((H, VW, T), f32),
            pltpu.VMEM((VW, H * T), bf16),
            pltpu.VMEM((H, T, VW), bf16),
            pltpu.VMEM((H, 4, 8, T), f32),
            pltpu.VMEM((H, 13, 8, T), f32),
            pltpu.VMEM((H, 4, 4, 4, R, WIDTH), bf16),
            pltpu.VMEM((H, 4, 4, 4, R, WIDTH), bf16),
            pltpu.VMEM((H, 4, 4, 4, R, WIDTH), bf16),
            pltpu.VMEM((H, 4, 4, R, WIDTH), bf16),
            pltpu.VMEM((H, 4, 4, R, WIDTH), bf16),
            pltpu.VMEM((H, 4, 4, R, WIDTH), bf16),
            pltpu.VMEM((H, 4, 4, R, WIDTH), bf16),
            pltpu.VMEM((H, 4, R, WIDTH), bf16),
            pltpu.VMEM((H, 4, R, WIDTH), bf16),
            pltpu.VMEM((H, 4, R, WIDTH), bf16),
            pltpu.VMEM((H, 4, R, WIDTH), f32),
            pltpu.VMEM((H, 3, R, WIDTH), f32),
            dma((6,)),
            dma((H,)),
            dma((H, 3, 7)),
            dma((H,)),
            dma((H,)),
            dma((H, 3)),
            dma((H, 3)),
            dma((H,)),
            dma((H, 4)),
            dma((H, 3)),
            dma((H, 3, 7)),
            dma,
        ],
        compiler_params=pltpu.CompilerParams(
            collective_id=0, has_side_effects=True, vmem_limit_bytes=62 * 2**20
        ),
        cost_estimate=pl.CostEstimate(flops=4 * 2 * 512 * 512 * 8192, bytes_accessed=3 * 2**23, transcendentals=2**20),
        name="head_step",
    )(hidden, ref_hidden, w_policy, w_ref, tok)


def solution(mesh):
    placed = (
        P("section", "tensor"),
        P("section", "tensor"),
        P(("section", "tensor"), None),
        P(("section", "tensor"), None),
        P(),
        P(),
        P(),
    )
    return jax.shard_map(
        shards,
        mesh=mesh,
        in_specs=placed,
        out_specs=(P("section", "tensor"), P(("section", "tensor"), None)),
        check_vma=False,
    )
```

```python
import functools

import jax
import jax.numpy as jnp
from jax import lax
from jax.experimental import pallas as pl
from jax.experimental.pallas import tpu as pltpu
from jax.sharding import PartitionSpec as P

MESH = pl.DeviceIdType.MESH
bf16, f32 = jnp.bfloat16, jnp.float32

loss_scale = 4.0
penalty_weight = 0.2

R = 32
WIDTH = 1024
T = 16 * R
VW = 512
X, Y, Z = 0, 1, 2
ORDERS = ((X, Y, Z), (Y, Z, X), (Z, X, Y))
GATHER = (
    ((0, 0, 32, 0, 384), (1, 0, 32, 384, 384), (2, 0, 32, 768, 256)),
    ((0, 0, 32, 1024, 256), (1, 0, 32, 1280, 256), (2, 0, 32, 1536, 384), (0, 0, 16, 1920, 128), (1, 16, 16, 1920, 128)),
)
REDUCE = ((0, 0, 32, 0, 256), (1, 0, 32, 256, 384), (2, 0, 32, 640, 384))
ROUNDS, PARTS = 2, 5
ALL = slice(None)
LOW, HIGH = slice(0, 2), slice(2, 4)


def wrap(i):
    return lax.rem(i + 4, 4)


def pick(ref, lead, axes, where, part):
    index = tuple(lead)
    for axis in axes:
        index += (where.get(axis, ALL),)
    return ref.at[index + (pl.ds(part[1], part[2]), pl.ds(part[3], part[4]))]


def kernel(
    hid, rhid, w_hbm, wr_hbm, ids_ref, mask_ref, adv_ref, out_h, out_w,
    g, w, wr, lg, rlg, gv, gt, st_s, st_r,
    fw, rl, rr, t3, fw2, rl2, rr2, t2, r1,
    load_sem, ag_send, ag_recv, dd_send, dd_recv, st_send, st_recv,
    y_send, y_recv, rs_send, rs3, rs2, rs1,
):
    section, tensor = lax.axis_index("section"), lax.axis_index("tensor")
    x, c = tensor // 2, lax.rem(tensor, 2)
    y, z = section // 4, lax.rem(section, 4)
    me = (x, y, z)
    offset = (section * 8 + tensor) * VW

    def device(dx=0, dy=0, dz=0, dc=0):
        return (
            lax.rem(y + dy + 4, 4) * 4 + lax.rem(z + dz + 4, 4),
            lax.rem(x + dx + 4, 4) * 2 + lax.rem(c + dc, 2),
        )

    def along(axis, k):
        step = [0, 0, 0]
        step[axis] = k
        return device(*step)

    def send(src, dst, ssem, rsem, to):
        pltpu.make_async_remote_copy(
            src_ref=src, dst_ref=dst, send_sem=ssem, recv_sem=rsem, device_id=to, device_id_type=MESH
        ).start()

    def wait(ref, sem):
        pltpu.make_async_copy(ref, ref, sem).wait()

    tensor_peers = [(kx, kc) for kx in range(4) for kc in range(2) if (kx, kc) != (0, 0)]
    groups = (
        [dict(dx=kx, dc=kc) for kx, kc in tensor_peers],
        [dict(dy=ky, dz=kz) for ky in range(4) for kz in range(4) if (ky, kz) != (0, 0)],
    )
    starts = (0, 7)
    peers = [peer for group in groups for peer in group]

    loads = [
        pltpu.make_async_copy(src, g.at[c, x, y, z, :, pl.ds(m * WIDTH, WIDTH)], load_sem.at[m])
        for m, src in enumerate((hid, rhid))
    ]
    for copy in loads:
        copy.start()
    barrier = pltpu.get_barrier_semaphore()
    for peer in peers:
        pl.semaphore_signal(barrier, inc=1, device_id=device(**peer), device_id_type=MESH)
    for copy in loads:
        copy.wait()
    pl.semaphore_wait(barrier, len(peers))

    def weights_start():
        for i in range(8):
            cols = pl.ds(i * WIDTH, WIDTH)
            pltpu.make_async_copy(w_hbm.at[:, cols], w.at[i], load_sem.at[2]).start()
        for i in range(8):
            cols = pl.ds(i * WIDTH, WIDTH)
            pltpu.make_async_copy(wr_hbm.at[:, :, :, cols], wr.at[i], load_sem.at[3]).start()

    def ag_part(part, where):
        return pick(g, (c,), (X, Y, Z), where, part)

    def ag_send_part(q, i, where, axis, k, event):
        part = ag_part(GATHER[q][i], where)
        send(part, part, ag_send, ag_recv.at[q, i, event], along(axis, k))

    def ag_core(q, i, where):
        part = ag_part(GATHER[q][i], where)
        send(part, part, dd_send, dd_recv.at[q], device(dc=1))

    def ag_wait(q, i, event, where):
        wait(ag_part(GATHER[q][i], where), ag_recv.at[q, i, event])

    def parts_of(q):
        return [(i,) + ORDERS[part[0]] for i, part in enumerate(GATHER[q])]

    one_line, two_lines, four_lines = {X: 0, Y: 0}, {X: 0, Y: slice(0, 2)}, {X: 0}

    def ag0(q):
        for i, a1, a2, a3 in parts_of(q):
            for k in (1, 3, 2):
                ag_send_part(q, i, {a1: me[a1], a2: me[a2], a3: me[a3]}, a1, k, 0)
            for axis, event in ((a2, 1), (a3, 3)):
                for k in (1, 3):
                    ag_send_part(q, i, {a1: me[a1], a2: me[a2], a3: me[a3]}, axis, k, event)

    def ag1(q):
        for i, a1, a2, a3 in parts_of(q):
            ag_wait(q, i, 0, {X: 0, Y: 0, Z: slice(0, 3)})
            line = {a2: me[a2], a3: me[a3]}
            for j in (1, 3, 2):
                block = {a1: wrap(me[a1] + j), **line}
                for axis, event in ((a2, 1), (a3, 3)):
                    for k in (1, 3):
                        ag_send_part(q, i, block, axis, k, event)

    def ag2(q):
        for i, a1, a2, a3 in parts_of(q):
            m2, m3 = me[a2], me[a3]
            ag_wait(q, i, 1, two_lines)
            left, right = wrap(m2 - 1), wrap(m2 + 1)
            ag_send_part(q, i, {a1: LOW, a2: left, a3: m3}, a2, 1, 2)
            ag_send_part(q, i, {a1: HIGH, a2: right, a3: m3}, a2, 3, 2)
            for j in (left, right):
                for k in (1, 3):
                    ag_send_part(q, i, {a2: j, a3: m3}, a3, k, 4)

    def ag_last(q, i, lines, event, waited):
        a1, a2, a3 = ORDERS[GATHER[q][i][0]]
        left, right = wrap(me[a3] - 1), wrap(me[a3] + 1)
        ag_wait(q, i, event, waited)
        for j in lines:
            ag_send_part(q, i, {a1: LOW, a2: j, a3: left}, a3, 1, event + 3)
            ag_send_part(q, i, {a1: HIGH, a2: j, a3: right}, a3, 3, event + 3)
        for j in lines:
            ag_core(q, i, {a2: j, a3: left})
            ag_core(q, i, {a2: j, a3: right})

    def ag3(q):
        for i, a1, a2, a3 in parts_of(q):
            ag_last(q, i, (me[a2],), 3, two_lines)

    def ag4(q):
        for i, a1, a2, a3 in parts_of(q):
            ag_wait(q, i, 2, one_line)
            line = {a2: wrap(me[a2] + 2), a3: me[a3]}
            for k in (1, 3):
                ag_send_part(q, i, line, a3, k, 5)
            ag_core(q, i, {a3: me[a3]})

    def ag5(q):
        for i, a1, a2, a3 in parts_of(q):
            ag_last(q, i, (wrap(me[a2] - 1), wrap(me[a2] + 1)), 4, four_lines)

    def ag6(q):
        for i, a1, a2, a3 in parts_of(q):
            ag_last(q, i, (wrap(me[a2] + 2),), 5, two_lines)

    def ag7(q):
        for i, a1, a2, a3 in parts_of(q):
            far = wrap(me[a3] + 2)
            ag_wait(q, i, 6, one_line)
            ag_core(q, i, {a2: me[a2], a3: far})
            ag_wait(q, i, 7, two_lines)
            ag_core(q, i, {a2: wrap(me[a2] - 1), a3: far})
            ag_core(q, i, {a2: wrap(me[a2] + 1), a3: far})

    def ag8(q):
        for i, a1, a2, a3 in parts_of(q):
            far = wrap(me[a3] + 2)
            ag_wait(q, i, 8, one_line)
            ag_core(q, i, {a2: wrap(me[a2] + 2), a3: far})

    def ag_core_wait(q):
        wait(g.at[1 - c, :, :, :, :, pl.ds(q * WIDTH, WIDTH)], dd_recv.at[q])

    def logits(m, core, first, last):
        def step(i, carry):
            rows = g[core, i, :, :, :, m * WIDTH:(m + 1) * WIDTH].reshape(T, WIDTH)
            weights, acc = (w, lg) if m == 0 else (wr, rlg)
            acc[...] += lax.dot_general(
                weights[i * 2 + core].reshape(VW, WIDTH), rows, (((1,), (1,)), ((), ())), preferred_element_type=f32
            )
            return carry

        lax.fori_loop(first, last, step, 0)

    def clear():
        lg[...] = jnp.zeros((VW, T), f32)
        rlg[...] = jnp.zeros((VW, T), f32)

    def local_stats():
        l, rf = lg[...], rlg[...]
        m = jnp.max(l, axis=0, keepdims=True)
        rm = jnp.max(rf, axis=0, keepdims=True)
        lm, rfm = l - m, rf - rm
        e = jnp.exp(lm)
        mass = jnp.sum(e, axis=0, keepdims=True)
        rmass = jnp.sum(jnp.exp(rfm), axis=0, keepdims=True)
        d = jnp.sum(e * (lm - rfm), axis=0, keepdims=True)
        st_s[0] = jnp.concatenate([m, mass, rm, rmass, d, d, d, d], axis=0)

    def stats_send(phase):
        for i, peer in enumerate(groups[phase]):
            send(
                st_s.at[phase], st_r.at[starts[phase] + i],
                st_send.at[phase], st_recv.at[phase], device(**peer),
            )

    def stats_wait(phase):
        n = len(groups[phase])
        wait(st_r.at[pl.ds(starts[phase], n)], st_recv.at[phase])
        terms = [st_s[phase]] + [st_r[starts[phase] + i] for i in range(n)]
        m = functools.reduce(jnp.maximum, [a[0:1] for a in terms])
        rm = functools.reduce(jnp.maximum, [a[2:3] for a in terms])
        mass, rmass, d = 0.0, 0.0, 0.0
        for a in terms:
            dm, drm = a[0:1] - m, a[2:3] - rm
            scale = jnp.exp(dm)
            mass += scale * a[1:2]
            rmass += jnp.exp(drm) * a[3:4]
            d += scale * (a[4:5] + a[1:2] * (dm - drm))
        st_s[phase + 1] = jnp.concatenate([m, mass, rm, rmass, d, d, d, d], axis=0)

    def grads():
        a = st_s[2]
        m, mass, rm, rmass, d = a[0:1], a[1:2], a[2:3], a[3:4], a[4:5]
        ln, rln = jnp.log(mass), jnp.log(rmass)
        divergence = d / mass - ln + rln
        weight = loss_scale * mask_ref[...].astype(f32)
        adv = adv_ref[...]
        place = ids_ref[...] - offset

        def step(i, carry):
            rows = pl.multiple_of(i * 128, 128)
            lp = (lg[pl.ds(rows, 128), :] - m) - ln
            rlp = (rlg[pl.ds(rows, 128), :] - rm) - rln
            p = jnp.exp(lp)
            entry = rows + lax.broadcasted_iota(jnp.int32, (128, T), 0)
            target = (entry == place).astype(f32)
            value = weight * (adv * (p - target) + penalty_weight * p * (lp - rlp - divergence))
            gv[pl.ds(rows, 128), :] = value.astype(bf16)
            gt[:, pl.ds(rows, 128)] = value.T.astype(bf16)
            return carry

        lax.fori_loop(0, VW // 128, step, 0)

    HALF = WIDTH // 2

    turns = (wrap(x + 2), wrap(x + 1), wrap(x - 1), x)

    def products_other(k):
        i = turns[k]
        for n in range(2):
            cols = slice(n * HALF, (n + 1) * HALF)
            rows = jnp.dot(gt[...], w[i * 2 + 1 - c, :, cols], preferred_element_type=f32)
            wr[i, :, :, :, cols] = rows.astype(bf16).reshape(4, 4, R, HALF)
        send(wr.at[i], g.at[c, i, :, :, :, pl.ds(WIDTH, WIDTH)], y_send, y_recv.at[k], device(dc=1))

    def products_own(k):
        i = turns[k]
        wait(g.at[1 - c, i, :, :, :, pl.ds(WIDTH, WIDTH)], y_recv.at[k])
        for n in range(2):
            cols = slice(n * HALF, (n + 1) * HALF)
            rows = jnp.dot(gt[...], w[i * 2 + c, :, cols], preferred_element_type=f32)
            theirs = g[1 - c, i, :, :, :, WIDTH + n * HALF:WIDTH + (n + 1) * HALF]
            rows += theirs.reshape(T, HALF).astype(f32)
            wr[4 + i, :, :, :, cols] = rows.astype(bf16).reshape(4, 4, R, HALF)

    def order(r):
        a1, a2, a3 = ORDERS[r]
        plane = tuple(a for a in (X, Y, Z) if a != a3)
        at = lambda ref, where: pick(ref, (), plane, where, REDUCE[r])
        line = lambda ref, where: pick(ref, (), (a1,), where, REDUCE[r])

        def mine(where):
            where = dict(where)
            j = where.get(X, ALL)
            where[X] = j + 4 if not isinstance(j, slice) else slice(4 + (j.start or 0), 4 + (j.stop or 4))
            return pick(wr, (), (X, Y, Z), where, REDUCE[r])

        return a1, a2, a3, at, line, mine

    def add(place, other):
        place[...] = (place[...].astype(f32) + other[...].astype(f32)).astype(bf16)

    def rs3_start(k):
        i, ss = turns[k], rs_send.at[0]
        a1, a2, a3, at, line, mine = order(0)
        right, left, far = wrap(z + 1), wrap(z - 1), wrap(z + 2)
        if k % 2 == 0:
            send(mine({X: i, Z: far}), at(fw, {X: i}), ss, rs3.at[0, 0, k], along(Z, 1))
            send(mine({X: i, Z: left}), at(rr, {X: i}), ss, rs3.at[0, 1, 0], along(Z, 3))
        else:
            send(mine({X: i, Z: far}), at(fw, {X: i}), ss, rs3.at[0, 0, k], along(Z, 3))
            send(mine({X: i, Z: right}), at(rl, {X: i}), ss, rs3.at[0, 1, 0], along(Z, 1))
        a1, a2, a3, at, line, mine = order(2)
        right, left, far = wrap(y + 1), wrap(y - 1), wrap(y + 2)
        send(mine({X: i, Y: far, Z: LOW}), at(fw, {X: i, Z: LOW}), ss, rs3.at[2, 0, k], along(Y, 1))
        send(mine({X: i, Y: far, Z: HIGH}), at(fw, {X: i, Z: HIGH}), ss, rs3.at[2, 0, k], along(Y, 3))
        send(mine({X: i, Y: right, Z: HIGH}), at(rl, {X: i, Z: HIGH}), ss, rs3.at[2, 1, k], along(Y, 1))
        send(mine({X: i, Y: left, Z: LOW}), at(rr, {X: i, Z: LOW}), ss, rs3.at[2, 1, k], along(Y, 3))
        a1, a2, a3, at, line, mine = order(1)
        if k == 0:
            send(mine({X: i, Y: LOW}), at(fw, {Y: LOW}), ss, rs3.at[1, 0, 0], along(X, 1))
            send(mine({X: i, Y: HIGH}), at(fw, {Y: HIGH}), ss, rs3.at[1, 0, 0], along(X, 3))
        elif k == 1:
            send(mine({X: i, Y: HIGH}), at(rl, {Y: HIGH}), ss, rs3.at[1, 1, 0], along(X, 1))
        elif k == 2:
            send(mine({X: i, Y: LOW}), at(rr, {Y: LOW}), ss, rs3.at[1, 1, 0], along(X, 3))

    def rs3_middle(k):
        i, ss = turns[k], rs_send.at[0]
        a1, a2, a3, at, line, mine = order(0)
        place = at(fw, {X: i})
        wait(place, rs3.at[0, 0, k])
        to, step, dst = (wrap(z + 1), 1, rl) if k % 2 == 0 else (wrap(z - 1), 3, rr)
        add(place, mine({X: i, Z: to}))
        send(place, at(dst, {X: i}), ss, rs3.at[0, 2, 0], along(Z, step))
        a1, a2, a3, at, line, mine = order(2)
        wait(at(fw, {X: i}), rs3.at[2, 0, k])
        for part, to, step, dst in ((LOW, wrap(y + 1), 1, rl), (HIGH, wrap(y - 1), 3, rr)):
            place = at(fw, {X: i, Z: part})
            add(place, mine({X: i, Y: to, Z: part}))
            send(place, at(dst, {X: i, Z: part}), ss, rs3.at[2, 2, k], along(Y, step))

    def rs3_middle_x():
        a1, a2, a3, at, line, mine = order(1)
        wait(at(fw, {}), rs3.at[1, 0, 0])
        for part, to, step, dst in ((LOW, turns[1], 1, rl), (HIGH, turns[2], 3, rr)):
            place = at(fw, {Y: part})
            add(place, mine({X: to, Y: part}))
            send(place, at(dst, {Y: part}), rs_send.at[0], rs3.at[1, 2, 0], along(X, step))

    def summed(at, where, own):
        total = own[...].astype(f32) + at(rl, where)[...].astype(f32) + at(rr, where)[...].astype(f32)
        at(t3, where)[...] = total.astype(bf16)

    def rs3_end_lines(k):
        i, ss = turns[k], rs_send.at[1]
        a1, a2, a3, at, line, mine = order(2)
        wait(at(rl, {X: i}), rs3.at[2, 1, k])
        wait(at(rr, {X: i}), rs3.at[2, 2, k])
        summed(at, {X: i}, mine({X: i, Y: y}))
        if k == 0:
            send(at(t3, {X: i, Z: LOW}), line(fw2, {Z: LOW}), ss, rs2.at[2, 0], along(X, 1))
            send(at(t3, {X: i, Z: HIGH}), line(fw2, {Z: HIGH}), ss, rs2.at[2, 0], along(X, 3))
        elif k == 1:
            send(at(t3, {X: i, Z: HIGH}), line(rl2, {Z: HIGH}), ss, rs2.at[2, 1], along(X, 1))
        elif k == 2:
            send(at(t3, {X: i, Z: LOW}), line(rr2, {Z: LOW}), ss, rs2.at[2, 1], along(X, 3))

    def rs3_end(r):
        ss = rs_send.at[1]
        a1, a2, a3, at, line, mine = order(r)
        wait(at(rl, {}), rs3.at[r, 1, 0])
        wait(at(rr, {}), rs3.at[r, 2, 0])
        summed(at, {}, mine({a3: me[a3]}))
        far, right, left = wrap(me[a2] + 2), wrap(me[a2] + 1), wrap(me[a2] - 1)
        send(at(t3, {a1: LOW, a2: far}), line(fw2, {a1: LOW}), ss, rs2.at[r, 0], along(a2, 1))
        send(at(t3, {a1: HIGH, a2: far}), line(fw2, {a1: HIGH}), ss, rs2.at[r, 0], along(a2, 3))
        send(at(t3, {a1: HIGH, a2: right}), line(rl2, {a1: HIGH}), ss, rs2.at[r, 1], along(a2, 1))
        send(at(t3, {a1: LOW, a2: left}), line(rr2, {a1: LOW}), ss, rs2.at[r, 1], along(a2, 3))

    def rs2_middle(r):
        a1, a2, a3, at, line, mine = order(r)
        wait(line(fw2, {}), rs2.at[r, 0])
        for part, to, step, dst in ((LOW, wrap(me[a2] + 1), 1, rl2), (HIGH, wrap(me[a2] - 1), 3, rr2)):
            place = line(fw2, {a1: part})
            add(place, at(t3, {a1: part, a2: to}))
            send(place, line(dst, {a1: part}), rs_send.at[1], rs2.at[r, 2], along(a2, step))

    def rs2_end(r):
        a1, a2, a3, at, line, mine = order(r)
        wait(line(rl2, {}), rs2.at[r, 1])
        wait(line(rr2, {}), rs2.at[r, 2])
        total = at(t3, {a2: me[a2]})[...].astype(f32) + line(rl2, {})[...].astype(f32)
        line(t2, {})[...] = total + line(rr2, {})[...].astype(f32)
        for k in (1, 2, 3):
            send(
                line(t2, {a1: wrap(me[a1] + k)}), line(r1, {a1: k - 1}), rs_send.at[2], rs1.at[r], along(a1, k)
            )

    def rs1_end(r):
        a1, a2, a3, at, line, mine = order(r)
        _, row, rows, col, cols = REDUCE[r]
        wait(line(r1, {}), rs1.at[r])
        total = line(t2, {a1: me[a1]})[...]
        for k in range(3):
            total += line(r1, {a1: k})[...]
        out_h[row:row + rows, col:col + cols] = total

    def head(first, last):
        def step(i, carry):
            rows = g[lax.rem(i, 2), i // 2, :, :, :, 0:WIDTH].reshape(T, WIDTH)
            total = jnp.dot(gv[...], rows, preferred_element_type=f32)
            out_w[:, pl.ds(pl.multiple_of(i * WIDTH, WIDTH), WIDTH)] = total.astype(bf16)
            return carry

        lax.fori_loop(first, last, step, 0)

    def weights_wait(m):
        ref = (w, wr)[m]
        wait(ref, load_sem.at[2 + m])

    def drain():
        wait(out_w.at[:, pl.ds(0, 63 * 128)], ag_send)
        wait(g.at[c], dd_send)
        for phase in range(2):
            n = len(groups[phase])
            wait(st_r.at[pl.ds(starts[phase], n)], st_send.at[phase])
        wait(wr.at[pl.ds(0, 4)], y_send)
        wait(wr.at[pl.ds(0, 3)], rs_send.at[0])
        wait(wr.at[0, pl.ds(0, 3)], rs_send.at[1])
        wait(t2.at[pl.ds(0, 3)], rs_send.at[2])

    ag0(0)
    ag0(1)
    weights_start()
    clear()
    for step in (ag1, ag2, ag3, ag4, ag5, ag6, ag7, ag8):
        step(0)
        step(1)
    weights_wait(0)
    logits(0, c, 0, 4)
    weights_wait(1)
    logits(1, c, 0, 4)
    ag_core_wait(0)
    logits(0, 1 - c, 0, 4)
    ag_core_wait(1)
    logits(1, 1 - c, 0, 4)
    local_stats()
    stats_send(0)
    stats_wait(0)
    stats_send(1)
    stats_wait(1)
    grads()
    products_other(0)
    products_other(1)
    products_own(0)
    rs3_start(0)
    products_other(2)
    products_own(1)
    rs3_start(1)
    products_other(3)
    products_own(2)
    rs3_start(2)
    rs3_middle(0)
    products_own(3)
    rs3_start(3)
    rs3_middle(1)
    rs3_middle_x()
    head(0, 1)
    rs3_middle(2)
    head(1, 2)
    rs3_middle(3)
    head(2, 4)
    rs3_end_lines(0)
    rs3_end_lines(1)
    head(4, 5)
    rs3_end_lines(2)
    rs3_end(1)
    head(5, 6)
    rs2_middle(2)
    rs3_end_lines(3)
    rs3_end(0)
    rs2_middle(1)
    rs2_end(2)
    head(6, 7)
    rs2_middle(0)
    rs2_end(1)
    rs2_end(0)
    head(7, 8)
    rs1_end(2)
    rs1_end(1)
    rs1_end(0)
    drain()


def shards(hidden, ref_hidden, w_policy, w_ref, token_ids, loss_mask, advantages):
    any_space = pl.BlockSpec(memory_space=pl.ANY)
    vmem = pl.BlockSpec(memory_space=pltpu.VMEM)
    dma = pltpu.SemaphoreType.DMA
    return pl.pallas_call(
        kernel,
        out_shape=(
            pltpu.VMEM((R, WIDTH), f32),
            pltpu.VMEM((VW, 8 * WIDTH), bf16),
        ),
        in_specs=[any_space] * 4 + [vmem] * 3,
        out_specs=(vmem, vmem),
        scratch_shapes=[
            pltpu.VMEM((2, 4, 4, 4, R, 2 * WIDTH), bf16),
            pltpu.VMEM((8, VW, WIDTH), bf16),
            pltpu.VMEM((8, 4, 4, R, WIDTH), bf16),
            pltpu.VMEM((VW, T), f32),
            pltpu.VMEM((VW, T), f32),
            pltpu.VMEM((VW, T), bf16),
            pltpu.VMEM((T, VW), bf16),
            pltpu.VMEM((3, 8, T), f32),
            pltpu.VMEM((22, 8, T), f32),
            pltpu.VMEM((4, 4, R, WIDTH), bf16),
            pltpu.VMEM((4, 4, R, WIDTH), bf16),
            pltpu.VMEM((4, 4, R, WIDTH), bf16),
            pltpu.VMEM((4, 4, R, WIDTH), bf16),
            pltpu.VMEM((4, R, WIDTH), bf16),
            pltpu.VMEM((4, R, WIDTH), bf16),
            pltpu.VMEM((4, R, WIDTH), bf16),
            pltpu.VMEM((4, R, WIDTH), f32),
            pltpu.VMEM((3, R, WIDTH), f32),
            dma((4,)),
            dma,
            dma((ROUNDS, PARTS, 9)),
            dma,
            dma((ROUNDS,)),
            dma((2,)),
            dma((2,)),
            dma,
            dma((4,)),
            dma((3,)),
            dma((3, 3, 4)),
            dma((3, 3)),
            dma((3,)),
        ],
        compiler_params=pltpu.CompilerParams(
            collective_id=0, has_side_effects=True, vmem_limit_bytes=46 * 2**20
        ),
        cost_estimate=pl.CostEstimate(flops=4 * 2 * 512 * 512 * 8192, bytes_accessed=3 * 2**23, transcendentals=2**20),
        name="head_step",
    )(
        hidden, ref_hidden, w_policy, w_ref.reshape(4, 4, R, 8 * WIDTH),
        token_ids.reshape(1, T), loss_mask.reshape(1, T), advantages.reshape(1, T),
    )


def solution(mesh):
    placed = (
        P("section", "tensor"),
        P("section", "tensor"),
        P(("section", "tensor"), None),
        P(("section", "tensor"), None),
        P(),
        P(),
        P(),
    )
    return jax.shard_map(
        shards,
        mesh=mesh,
        in_specs=placed,
        out_specs=(P("section", "tensor"), P(("section", "tensor"), None)),
        check_vma=False,
    )
```

```python
import functools

import jax
import jax.numpy as jnp
from jax import lax
from jax.experimental import pallas as pl
from jax.experimental.pallas import tpu as pltpu
from jax.sharding import PartitionSpec as P

MESH = pl.DeviceIdType.MESH
bf16, f32 = jnp.bfloat16, jnp.float32

loss_scale = 4.0
penalty_weight = 0.2

R = 32
WIDTH = 1024
T = 16 * R
VW = 512
X, Y, Z = 0, 1, 2
ORDERS = ((X, Y, Z), (Y, Z, X), (Z, X, Y))
SUM_ORDERS = ((Y, X, Z), (Z, Y, X), (Z, X, Y))
GATHER = (
    ((0, 0, 32, 0, 384), (2, 0, 32, 384, 384), (1, 0, 32, 768, 256)),
    ((0, 0, 32, 1024, 256), (2, 0, 32, 1280, 256), (0, 0, 16, 1536, 128), (2, 16, 16, 1536, 128), (1, 0, 32, 1664, 384)),
)
EARLY = (768, 640)
REDUCE = ((0, 0, 32, 0, 384), (1, 0, 32, 384, 256), (2, 0, 32, 640, 384))
ROUNDS, PARTS = 2, 5
ALL = slice(None)
LOW, HIGH = slice(0, 2), slice(2, 4)


def wrap(i):
    return lax.rem(i + 4, 4)


def two_rows(a):
    return jnp.concatenate([a[:, :T // 2], a[:, T // 2:]], axis=0)


def one_row(a):
    return jnp.concatenate([a[0:1], a[1:2]], axis=1)


def pick(ref, lead, axes, where, part):
    index = tuple(lead)
    for axis in axes:
        index += (where.get(axis, ALL),)
    return ref.at[index + (pl.ds(part[1], part[2]), pl.ds(part[3], part[4]))]


def kernel(
    hid, rhid, w_hbm, wr_hbm, ids_ref, mask_ref, adv_ref, out_h, out_w,
    g, w, wr, lg, rlg, gv, gt, st_s, st_r,
    fw, rl, rr, t3, fw2, rl2, rr2, t2, r1,
    load_sem, ag_send, ag_recv, dd_send, dd_recv, st_send, st_recv,
    y_send, y_recv, rs_send, rs3, rs2, rs1,
):
    section, tensor = lax.axis_index("section"), lax.axis_index("tensor")
    x, c = tensor // 2, lax.rem(tensor, 2)
    y, z = section // 4, lax.rem(section, 4)
    me = (x, y, z)
    offset = (section * 8 + tensor) * VW

    def device(dx=0, dy=0, dz=0, dc=0):
        return (
            lax.rem(y + dy + 4, 4) * 4 + lax.rem(z + dz + 4, 4),
            lax.rem(x + dx + 4, 4) * 2 + lax.rem(c + dc, 2),
        )

    def along(axis, k):
        step = [0, 0, 0]
        step[axis] = k
        return device(*step)

    def send(src, dst, ssem, rsem, to):
        pltpu.make_async_remote_copy(
            src_ref=src, dst_ref=dst, send_sem=ssem, recv_sem=rsem, device_id=to, device_id_type=MESH
        ).start()

    def wait(ref, sem):
        pltpu.make_async_copy(ref, ref, sem).wait()

    tensor_peers = [(kx, kc) for kx in range(4) for kc in range(2) if (kx, kc) != (0, 0)]
    groups = (
        [dict(dx=kx, dc=kc) for kx, kc in tensor_peers],
        [dict(dy=ky, dz=kz) for ky in range(4) for kz in range(4) if (ky, kz) != (0, 0)],
    )
    starts = (0, 7)
    peers = [peer for group in groups for peer in group]

    loads = [
        pltpu.make_async_copy(src, g.at[c, x, y, z, :, pl.ds(m * WIDTH, WIDTH)], load_sem.at[m])
        for m, src in enumerate((hid, rhid))
    ]
    for copy in loads:
        copy.start()
    barrier = pltpu.get_barrier_semaphore()
    for peer in peers:
        pl.semaphore_signal(barrier, inc=1, device_id=device(**peer), device_id_type=MESH)
    for copy in loads:
        copy.wait()
    pl.semaphore_wait(barrier, len(peers))

    def weights_start():
        for i in range(8):
            cols = pl.ds(i * WIDTH, WIDTH)
            pltpu.make_async_copy(w_hbm.at[:, cols], w.at[i], load_sem.at[2]).start()
        for i in range(8):
            cols = pl.ds(i * WIDTH, WIDTH)
            pltpu.make_async_copy(wr_hbm.at[:, :, :, cols], wr.at[i], load_sem.at[3]).start()

    def ag_part(part, where):
        return pick(g, (c,), (X, Y, Z), where, part)

    def ag_send_part(q, i, where, axis, k, event):
        part = ag_part(GATHER[q][i], where)
        send(part, part, ag_send, ag_recv.at[q, i, event], along(axis, k))

    def ag_core(q, i, where, plane):
        part = ag_part(GATHER[q][i], where)
        send(part, part, dd_send, dd_recv.at[q, i, plane], device(dc=1))

    def ag_wait(q, i, event, where):
        wait(ag_part(GATHER[q][i], where), ag_recv.at[q, i, event])

    def parts_of(q):
        return [(i,) + ORDERS[part[0]] for i, part in enumerate(GATHER[q])]

    one_line, two_lines, four_lines = {X: 0, Y: 0}, {X: 0, Y: slice(0, 2)}, {X: 0}

    def ag0(q):
        for i, a1, a2, a3 in parts_of(q):
            for k in (1, 3, 2):
                ag_send_part(q, i, {a1: me[a1], a2: me[a2], a3: me[a3]}, a1, k, 0)
            for axis, event in ((a2, 1), (a3, 3)):
                for k in (1, 3):
                    ag_send_part(q, i, {a1: me[a1], a2: me[a2], a3: me[a3]}, axis, k, event)

    def ag1(q):
        for i, a1, a2, a3 in parts_of(q):
            ag_wait(q, i, 0, {X: 0, Y: 0, Z: slice(0, 3)})
            line = {a2: me[a2], a3: me[a3]}
            for j in (1, 3, 2):
                block = {a1: wrap(me[a1] + j), **line}
                for axis, event in ((a2, 1), (a3, 3)):
                    for k in (1, 3):
                        ag_send_part(q, i, block, axis, k, event)

    def ag2(q):
        for i, a1, a2, a3 in parts_of(q):
            m2, m3 = me[a2], me[a3]
            ag_wait(q, i, 1, two_lines)
            left, right = wrap(m2 - 1), wrap(m2 + 1)
            ag_send_part(q, i, {a1: LOW, a2: left, a3: m3}, a2, 1, 2)
            ag_send_part(q, i, {a1: HIGH, a2: right, a3: m3}, a2, 3, 2)
            for j in (left, right):
                for k in (1, 3):
                    ag_send_part(q, i, {a2: j, a3: m3}, a3, k, 4)

    def ag_last(q, i, lines, event, waited):
        a1, a2, a3 = ORDERS[GATHER[q][i][0]]
        left, right = wrap(me[a3] - 1), wrap(me[a3] + 1)
        ag_wait(q, i, event, waited)
        for j in lines:
            ag_send_part(q, i, {a1: LOW, a2: j, a3: left}, a3, 1, event + 3)
            ag_send_part(q, i, {a1: HIGH, a2: j, a3: right}, a3, 3, event + 3)
        for j in lines:
            ag_core(q, i, {a2: j, a3: left}, 1)
            ag_core(q, i, {a2: j, a3: right}, 1)

    def ag3(q):
        for i, a1, a2, a3 in parts_of(q):
            ag_last(q, i, (me[a2],), 3, two_lines)

    def ag4(q):
        for i, a1, a2, a3 in parts_of(q):
            ag_wait(q, i, 2, one_line)
            line = {a2: wrap(me[a2] + 2), a3: me[a3]}
            for k in (1, 3):
                ag_send_part(q, i, line, a3, k, 5)
            ag_core(q, i, {a3: me[a3]}, 0)

    def ag5(q):
        for i, a1, a2, a3 in parts_of(q):
            ag_last(q, i, (wrap(me[a2] - 1), wrap(me[a2] + 1)), 4, four_lines)

    def ag6(q):
        for i, a1, a2, a3 in parts_of(q):
            ag_last(q, i, (wrap(me[a2] + 2),), 5, two_lines)

    def ag7(q):
        for i, a1, a2, a3 in parts_of(q):
            far = wrap(me[a3] + 2)
            ag_wait(q, i, 6, one_line)
            ag_core(q, i, {a2: me[a2], a3: far}, 2)
            ag_wait(q, i, 7, two_lines)
            ag_core(q, i, {a2: wrap(me[a2] - 1), a3: far}, 2)
            ag_core(q, i, {a2: wrap(me[a2] + 1), a3: far}, 2)

    def ag8(q):
        for i, a1, a2, a3 in parts_of(q):
            far = wrap(me[a3] + 2)
            ag_wait(q, i, 8, one_line)
            ag_core(q, i, {a2: wrap(me[a2] + 2), a3: far}, 2)

    def ag_core_wait(q, i, plane):
        planes = pl.ds(0, 2) if plane == 1 else 0
        wait(pick(g, (1 - c,), (X, Y, Z), {X: planes}, GATHER[q][i]), dd_recv.at[q, i, plane])

    def early_core_wait(plane):
        for q in range(ROUNDS):
            ag_core_wait(q, len(GATHER[q]) - 1, plane)

    def late_core_wait():
        for q in range(ROUNDS):
            for i in range(len(GATHER[q]) - 1):
                for plane in range(3):
                    ag_core_wait(q, i, plane)

    def logits(m, core, chips, first, last):
        rows = [g[core, i, :, :, :, m * WIDTH + first:m * WIDTH + last].reshape(T, last - first) for i in chips]
        if m == 0:
            weights = [w[i * 2 + core, :, first:last] for i in chips]
        else:
            weights = [wr[i * 2 + core, :, :, :, first:last].reshape(VW, last - first) for i in chips]
        acc = (lg, rlg)[m]
        acc[...] += lax.dot_general(
            jnp.concatenate(weights, axis=1), jnp.concatenate(rows, axis=1),
            (((1,), (1,)), ((), ())), preferred_element_type=f32,
        )

    def early_logits(core, first, count, stride=1):
        def step(j, carry):
            for m in range(2):
                logits(m, core, (wrap(x + first + stride * j),), EARLY[m], WIDTH)
            return carry

        lax.fori_loop(0, count, step, 0)

    def late_logits(m, core):
        logits(m, core, (0, 1, 2, 3), 0, EARLY[m])

    def clear():
        lg[...] = jnp.zeros((VW, T), f32)
        rlg[...] = jnp.zeros((VW, T), f32)

    def local_stats():
        l, rf = lg[...], rlg[...]
        m = jnp.max(l, axis=0, keepdims=True)
        rm = jnp.max(rf, axis=0, keepdims=True)
        lm, rfm = l - m, rf - rm
        e = jnp.exp(lm)
        mass = jnp.sum(e, axis=0, keepdims=True)
        rmass = jnp.sum(jnp.exp(rfm), axis=0, keepdims=True)
        d = jnp.sum(e * (lm - rfm), axis=0, keepdims=True)
        ln, rln = jnp.log(mass), jnp.log(rmass)
        lse, rlse, kl = two_rows(m + ln), two_rows(rm + rln), two_rows(d / mass - ln + rln)
        st_s[0] = jnp.concatenate([lse, rlse, kl, kl], axis=0)

    def stats_send(phase):
        for i, peer in enumerate(groups[phase]):
            send(
                st_s.at[phase], st_r.at[starts[phase] + i],
                st_send.at[phase], st_recv.at[phase], device(**peer),
            )

    def stats_wait(phase):
        n = len(groups[phase])
        wait(st_r.at[pl.ds(starts[phase], n)], st_recv.at[phase])
        terms = [st_s[phase]] + [st_r[starts[phase] + i] for i in range(n)]
        m = functools.reduce(jnp.maximum, [a[0:2] for a in terms])
        rm = functools.reduce(jnp.maximum, [a[2:4] for a in terms])
        shares = [jnp.exp(a[0:2] - m) for a in terms]
        mass = sum(shares)
        lse = m + jnp.log(mass)
        rlse = rm + jnp.log(sum(jnp.exp(a[2:4] - rm) for a in terms))
        kl = sum(e * (a[4:6] + (a[0:2] - lse) - (a[2:4] - rlse)) for e, a in zip(shares, terms)) / mass
        st_s[phase + 1] = jnp.concatenate([lse, rlse, kl, kl], axis=0)

    def grads():
        a = st_s[2]
        lse, rlse, divergence = one_row(a[0:2]), one_row(a[2:4]), one_row(a[4:6])
        weight = loss_scale * mask_ref[...].astype(f32)
        adv = adv_ref[...]
        place = ids_ref[...] - offset

        def step(i, carry):
            rows = pl.multiple_of(i * 128, 128)
            lp = lg[pl.ds(rows, 128), :] - lse
            rlp = rlg[pl.ds(rows, 128), :] - rlse
            p = jnp.exp(lp)
            entry = rows + lax.broadcasted_iota(jnp.int32, (128, T), 0)
            target = (entry == place).astype(f32)
            value = weight * (adv * (p - target) + penalty_weight * p * (lp - rlp - divergence))
            gv[pl.ds(rows, 128), :] = value.astype(bf16)
            gt[:, pl.ds(rows, 128)] = value.T.astype(bf16)
            return carry

        lax.fori_loop(0, VW // 128, step, 0)

    turns = (wrap(x + 2), wrap(x + 1), wrap(x - 1), x)

    def products_other(k):
        i = turns[k]
        rows = jnp.dot(gt[...], w[i * 2 + 1 - c], preferred_element_type=f32)
        wr[i] = rows.astype(bf16).reshape(4, 4, R, WIDTH)
        send(wr.at[i], g.at[c, i, :, :, :, pl.ds(WIDTH, WIDTH)], y_send, y_recv.at[k], device(dc=1))

    def products_own(k):
        i = turns[k]
        rows = jnp.dot(gt[...], w[i * 2 + c], preferred_element_type=f32)
        wait(g.at[1 - c, i, :, :, :, pl.ds(WIDTH, WIDTH)], y_recv.at[k])
        rows += g[1 - c, i, :, :, :, WIDTH:2 * WIDTH].reshape(T, WIDTH).astype(f32)
        wr[4 + i] = rows.astype(bf16).reshape(4, 4, R, WIDTH)

    def order(r):
        a1, a2, a3 = SUM_ORDERS[r]
        plane = tuple(a for a in (X, Y, Z) if a != a3)
        at = lambda ref, where: pick(ref, (), plane, where, REDUCE[r])
        line = lambda ref, where: pick(ref, (), (a1,), where, REDUCE[r])

        def mine(where):
            where = dict(where)
            j = where.get(X, ALL)
            where[X] = j + 4 if not isinstance(j, slice) else slice(4 + (j.start or 0), 4 + (j.stop or 4))
            return pick(wr, (), (X, Y, Z), where, REDUCE[r])

        return a1, a2, a3, at, line, mine

    def add(place, other):
        place[...] = (place[...].astype(f32) + other[...].astype(f32)).astype(bf16)

    def rs3_start(k):
        i, ss = turns[k], rs_send.at[0]
        for r in (0, 2):
            a1, a2, a3, at, line, mine = order(r)
            for part, step in ((LOW, 1), (HIGH, 3)):
                send(
                    mine({X: i, a3: wrap(me[a3] + 2), a1: part}), at(fw, {X: i, a1: part}),
                    ss, rs3.at[r, 0, k], along(a3, step),
                )
        if k == 0:
            a1, a2, a3, at, line, mine = order(1)
            for part, step in ((LOW, 1), (HIGH, 3)):
                send(mine({X: i, a1: part}), at(fw, {a1: part}), ss, rs3.at[1, 0, 0], along(X, step))

    def rs3_raw(k):
        i, ss = turns[k], rs_send.at[0]
        for r in (0, 2):
            a1, a2, a3, at, line, mine = order(r)
            for part, step, dst in ((HIGH, 1, rl), (LOW, 3, rr)):
                send(
                    mine({X: i, a3: wrap(me[a3] + step), a1: part}), at(dst, {X: i, a1: part}),
                    ss, rs3.at[r, 1, k], along(a3, step),
                )
        if k in (1, 2):
            a1, a2, a3, at, line, mine = order(1)
            part, step, dst = ((HIGH, 1, rl), (LOW, 3, rr))[k - 1]
            send(mine({X: i, a1: part}), at(dst, {a1: part}), ss, rs3.at[1, 1, 0], along(X, step))

    def rs3_middle(k):
        i, ss = turns[k], rs_send.at[0]
        for r in (0, 2):
            a1, a2, a3, at, line, mine = order(r)
            wait(at(fw, {X: i}), rs3.at[r, 0, k])
            for part, step, dst in ((LOW, 1, rl), (HIGH, 3, rr)):
                place = at(fw, {X: i, a1: part})
                add(place, mine({X: i, a3: wrap(me[a3] + step), a1: part}))
                send(place, at(dst, {X: i, a1: part}), ss, rs3.at[r, 2, k], along(a3, step))

    def rs3_middle_x():
        a1, a2, a3, at, line, mine = order(1)
        wait(at(fw, {}), rs3.at[1, 0, 0])
        for part, to, step, dst in ((LOW, turns[1], 1, rl), (HIGH, turns[2], 3, rr)):
            place = at(fw, {a1: part})
            add(place, mine({X: to, a1: part}))
            send(place, at(dst, {a1: part}), rs_send.at[0], rs3.at[1, 2, 0], along(X, step))

    def summed(at, where, own):
        total = own[...].astype(f32) + at(rl, where)[...].astype(f32) + at(rr, where)[...].astype(f32)
        at(t3, where)[...] = total.astype(bf16)

    def rs3_end_lines(k):
        i, ss = turns[k], rs_send.at[1]
        for r in (0, 2):
            a1, a2, a3, at, line, mine = order(r)
            wait(at(rl, {X: i}), rs3.at[r, 1, k])
            wait(at(rr, {X: i}), rs3.at[r, 2, k])
            summed(at, {X: i}, mine({X: i, a3: me[a3]}))
            if k == 0:
                send(at(t3, {X: i, a1: LOW}), line(fw2, {a1: LOW}), ss, rs2.at[r, 0], along(X, 1))
                send(at(t3, {X: i, a1: HIGH}), line(fw2, {a1: HIGH}), ss, rs2.at[r, 0], along(X, 3))
            elif k == 1:
                send(at(t3, {X: i, a1: HIGH}), line(rl2, {a1: HIGH}), ss, rs2.at[r, 1], along(X, 1))
            elif k == 2:
                send(at(t3, {X: i, a1: LOW}), line(rr2, {a1: LOW}), ss, rs2.at[r, 1], along(X, 3))

    def rs3_end(r):
        ss = rs_send.at[1]
        a1, a2, a3, at, line, mine = order(r)
        wait(at(rl, {}), rs3.at[r, 1, 0])
        wait(at(rr, {}), rs3.at[r, 2, 0])
        summed(at, {}, mine({a3: me[a3]}))
        far, right, left = wrap(me[a2] + 2), wrap(me[a2] + 1), wrap(me[a2] - 1)
        send(at(t3, {a1: LOW, a2: far}), line(fw2, {a1: LOW}), ss, rs2.at[r, 0], along(a2, 1))
        send(at(t3, {a1: HIGH, a2: far}), line(fw2, {a1: HIGH}), ss, rs2.at[r, 0], along(a2, 3))
        send(at(t3, {a1: HIGH, a2: right}), line(rl2, {a1: HIGH}), ss, rs2.at[r, 1], along(a2, 1))
        send(at(t3, {a1: LOW, a2: left}), line(rr2, {a1: LOW}), ss, rs2.at[r, 1], along(a2, 3))

    def rs2_middle(r):
        a1, a2, a3, at, line, mine = order(r)
        wait(line(fw2, {}), rs2.at[r, 0])
        for part, to, step, dst in ((LOW, wrap(me[a2] + 1), 1, rl2), (HIGH, wrap(me[a2] - 1), 3, rr2)):
            place = line(fw2, {a1: part})
            add(place, at(t3, {a1: part, a2: to}))
            send(place, line(dst, {a1: part}), rs_send.at[1], rs2.at[r, 2], along(a2, step))

    def rs2_end(r):
        a1, a2, a3, at, line, mine = order(r)
        wait(line(rl2, {}), rs2.at[r, 1])
        wait(line(rr2, {}), rs2.at[r, 2])
        total = at(t3, {a2: me[a2]})[...].astype(f32) + line(rl2, {})[...].astype(f32)
        line(t2, {})[...] = total + line(rr2, {})[...].astype(f32)
        for k in (1, 2, 3):
            send(
                line(t2, {a1: wrap(me[a1] + k)}), line(r1, {a1: k - 1}), rs_send.at[2], rs1.at[r], along(a1, k)
            )

    def rs1_end(r):
        a1, a2, a3, at, line, mine = order(r)
        _, row, rows, col, cols = REDUCE[r]
        wait(line(r1, {}), rs1.at[r])
        total = line(t2, {a1: me[a1]})[...]
        for k in range(3):
            total += line(r1, {a1: k})[...]
        out_h[row:row + rows, col:col + cols] = total

    def head(first, last):
        def step(i, carry):
            rows = g[lax.rem(i, 2), i // 2, :, :, :, 0:WIDTH].reshape(T, WIDTH)
            total = jnp.dot(gv[...], rows, preferred_element_type=f32)
            out_w[:, pl.ds(pl.multiple_of(i * WIDTH, WIDTH), WIDTH)] = total.astype(bf16)
            return carry

        lax.fori_loop(first, last, step, 0)

    def weights_wait(m):
        ref = (w, wr)[m]
        wait(ref, load_sem.at[2 + m])

    def drain():
        wait(out_w.at[:, pl.ds(0, 63 * 128)], ag_send)
        wait(g.at[c], dd_send)
        for phase in range(2):
            n = len(groups[phase])
            wait(st_r.at[pl.ds(starts[phase], n)], st_send.at[phase])
        wait(wr.at[pl.ds(0, 4)], y_send)
        wait(wr.at[pl.ds(0, 3)], rs_send.at[0])
        wait(wr.at[0, pl.ds(0, 3)], rs_send.at[1])
        wait(t2.at[pl.ds(0, 3)], rs_send.at[2])

    ag0(0)
    ag0(1)
    weights_start()
    clear()
    for step in (ag1, ag2, ag3, ag4):
        step(0)
        step(1)
    weights_wait(0)
    weights_wait(1)
    early_logits(c, 0, 1)
    ag5(0)
    ag5(1)
    early_core_wait(0)
    early_logits(1 - c, 0, 1)
    ag6(0)
    ag6(1)
    early_logits(c, 1, 2, 2)
    ag7(0)
    ag7(1)
    early_core_wait(1)
    early_logits(1 - c, 1, 2, 2)
    ag8(0)
    ag8(1)
    late_logits(0, c)
    late_logits(1, c)
    early_logits(c, 2, 1)
    early_core_wait(2)
    early_logits(1 - c, 2, 1)
    late_core_wait()
    late_logits(0, 1 - c)
    late_logits(1, 1 - c)
    local_stats()
    stats_send(0)
    stats_wait(0)
    stats_send(1)
    stats_wait(1)
    grads()
    products_other(0)
    products_other(1)
    products_own(0)
    rs3_start(0)
    products_other(2)
    products_own(1)
    rs3_start(1)
    rs3_raw(0)
    products_other(3)
    products_own(2)
    rs3_start(2)
    rs3_middle(0)
    rs3_raw(1)
    products_own(3)
    rs3_start(3)
    rs3_middle(1)
    rs3_raw(2)
    rs3_middle_x()
    rs3_raw(3)
    rs3_middle(2)
    head(0, 1)
    rs3_middle(3)
    head(1, 2)
    rs3_end_lines(0)
    head(2, 3)
    rs3_end_lines(1)
    rs3_end(1)
    head(3, 4)
    rs3_end_lines(2)
    rs2_middle(0)
    rs2_middle(2)
    rs2_middle(1)
    head(4, 6)
    rs3_end_lines(3)
    rs2_end(1)
    rs2_end(0)
    rs2_end(2)
    head(6, 8)
    rs1_end(1)
    rs1_end(0)
    rs1_end(2)
    drain()


def shards(hidden, ref_hidden, w_policy, w_ref, token_ids, loss_mask, advantages):
    any_space = pl.BlockSpec(memory_space=pl.ANY)
    vmem = pl.BlockSpec(memory_space=pltpu.VMEM)
    dma = pltpu.SemaphoreType.DMA
    return pl.pallas_call(
        kernel,
        out_shape=(
            pltpu.VMEM((R, WIDTH), f32),
            pltpu.VMEM((VW, 8 * WIDTH), bf16),
        ),
        in_specs=[any_space] * 4 + [vmem] * 3,
        out_specs=(vmem, vmem),
        scratch_shapes=[
            pltpu.VMEM((2, 4, 4, 4, R, 2 * WIDTH), bf16),
            pltpu.VMEM((8, VW, WIDTH), bf16),
            pltpu.VMEM((8, 4, 4, R, WIDTH), bf16),
            pltpu.VMEM((VW, T), f32),
            pltpu.VMEM((VW, T), f32),
            pltpu.VMEM((VW, T), bf16),
            pltpu.VMEM((T, VW), bf16),
            pltpu.VMEM((3, 8, T // 2), f32),
            pltpu.VMEM((22, 8, T // 2), f32),
            pltpu.VMEM((4, 4, R, WIDTH), bf16),
            pltpu.VMEM((4, 4, R, WIDTH), bf16),
            pltpu.VMEM((4, 4, R, WIDTH), bf16),
            pltpu.VMEM((4, 4, R, WIDTH), bf16),
            pltpu.VMEM((4, R, WIDTH), bf16),
            pltpu.VMEM((4, R, WIDTH), bf16),
            pltpu.VMEM((4, R, WIDTH), bf16),
            pltpu.VMEM((4, R, WIDTH), f32),
            pltpu.VMEM((3, R, WIDTH), f32),
            dma((4,)),
            dma,
            dma((ROUNDS, PARTS, 9)),
            dma,
            dma((ROUNDS, PARTS, 3)),
            dma((2,)),
            dma((2,)),
            dma,
            dma((4,)),
            dma((3,)),
            dma((3, 3, 4)),
            dma((3, 3)),
            dma((3,)),
        ],
        compiler_params=pltpu.CompilerParams(
            collective_id=0, has_side_effects=True, vmem_limit_bytes=46 * 2**20
        ),
        cost_estimate=pl.CostEstimate(flops=4 * 2 * 512 * 512 * 8192, bytes_accessed=3 * 2**23, transcendentals=2**20),
        name="head_step",
    )(
        hidden, ref_hidden, w_policy, w_ref.reshape(4, 4, R, 8 * WIDTH),
        token_ids.reshape(1, T), loss_mask.reshape(1, T), advantages.reshape(1, T),
    )


def solution(mesh):
    placed = (
        P("section", "tensor"),
        P("section", "tensor"),
        P(("section", "tensor"), None),
        P(("section", "tensor"), None),
        P(),
        P(),
        P(),
    )
    return jax.shard_map(
        shards,
        mesh=mesh,
        in_specs=placed,
        out_specs=(P("section", "tensor"), P(("section", "tensor"), None)),
        check_vma=False,
    )
```

```python
import functools

import jax
import jax.numpy as jnp
from jax import lax
from jax.experimental import pallas as pl
from jax.experimental.pallas import tpu as pltpu
from jax.sharding import PartitionSpec as P

MESH = pl.DeviceIdType.MESH
bf16, f32 = jnp.bfloat16, jnp.float32

loss_scale = 4.0
penalty_weight = 0.2

R = 32
WIDTH = 1024
T = 16 * R
VW = 512
X, Y, Z = 0, 1, 2
ORDERS = ((X, Y, Z), (Y, Z, X), (Z, X, Y))
SUM_ORDERS = ((Y, X, Z), (Z, Y, X), (Z, X, Y))
GATHER = (
    ((0, 0, 32, 0, 384), (2, 0, 32, 384, 384), (1, 0, 32, 768, 256)),
    ((0, 0, 32, 1024, 256), (2, 0, 32, 1280, 256), (0, 0, 16, 1536, 128), (2, 16, 16, 1536, 128), (1, 0, 32, 1664, 384)),
)
EARLY = (768, 640)
REDUCE = ((0, 0, 32, 0, 384), (1, 0, 32, 384, 256), (2, 0, 32, 640, 384))
ROUNDS, PARTS = 2, 5
ALL = slice(None)
LOW, HIGH = slice(0, 2), slice(2, 4)


def wrap(i):
    return lax.rem(i + 4, 4)


def two_rows(a):
    return jnp.concatenate([a[:, :T // 2], a[:, T // 2:]], axis=0)


def one_row(a):
    return jnp.concatenate([a[0:1], a[1:2]], axis=1)


def pick(ref, lead, axes, where, part):
    index = tuple(lead)
    for axis in axes:
        index += (where.get(axis, ALL),)
    return ref.at[index + (pl.ds(part[1], part[2]), pl.ds(part[3], part[4]))]


def kernel(
    hid, rhid, w_hbm, wr_hbm, ids_ref, mask_ref, adv_ref, out_h, out_w,
    g, w, wr, w2, lg, rlg, gv, gt, st_s, st_r,
    fw, rl, rr, t3, fw2, rl2, rr2, t2, r1,
    load_sem, ag_send, ag_recv, dd_send, dd_recv, st_send, st_recv,
    swap_send, swap_recv, rs_send, rs3, rs2, rs1,
):
    section, tensor = lax.axis_index("section"), lax.axis_index("tensor")
    x, c = tensor // 2, lax.rem(tensor, 2)
    y, z = section // 4, lax.rem(section, 4)
    me = (x, y, z)
    offset = (section * 8 + tensor) * VW

    def device(dx=0, dy=0, dz=0, dc=0):
        return (
            lax.rem(y + dy + 4, 4) * 4 + lax.rem(z + dz + 4, 4),
            lax.rem(x + dx + 4, 4) * 2 + lax.rem(c + dc, 2),
        )

    def along(axis, k):
        step = [0, 0, 0]
        step[axis] = k
        return device(*step)

    def send(src, dst, ssem, rsem, to):
        pltpu.make_async_remote_copy(
            src_ref=src, dst_ref=dst, send_sem=ssem, recv_sem=rsem, device_id=to, device_id_type=MESH
        ).start()

    def wait(ref, sem):
        pltpu.make_async_copy(ref, ref, sem).wait()

    tensor_peers = [(kx, kc) for kx in range(4) for kc in range(2) if (kx, kc) != (0, 0)]
    groups = (
        [dict(dx=kx, dc=kc) for kx, kc in tensor_peers],
        [dict(dy=ky, dz=kz) for ky in range(4) for kz in range(4) if (ky, kz) != (0, 0)],
    )
    starts = (0, 7)
    peers = [peer for group in groups for peer in group]

    loads = [
        pltpu.make_async_copy(src, g.at[c, x, y, z, :, pl.ds(m * WIDTH, WIDTH)], load_sem.at[m])
        for m, src in enumerate((hid, rhid))
    ]
    for copy in loads:
        copy.start()
    barrier = pltpu.get_barrier_semaphore()
    for peer in peers:
        pl.semaphore_signal(barrier, inc=1, device_id=device(**peer), device_id_type=MESH)
    for copy in loads:
        copy.wait()
    pl.semaphore_wait(barrier, len(peers))

    def weights_start():
        for i in range(8):
            cols = pl.ds(i * WIDTH, WIDTH)
            pltpu.make_async_copy(w_hbm.at[:, cols], w.at[i], load_sem.at[2]).start()
        for i in range(8):
            cols = pl.ds(i * WIDTH, WIDTH)
            pltpu.make_async_copy(wr_hbm.at[:, :, :, cols], wr.at[i], load_sem.at[3]).start()
        for i in range(4):
            cols = pl.ds(pl.multiple_of((i * 2 + 1 - c) * WIDTH, WIDTH), WIDTH)
            send(w_hbm.at[:, cols], w2.at[i], swap_send.at[0], swap_recv.at[0], device(dc=1))

    def ag_part(part, where):
        return pick(g, (c,), (X, Y, Z), where, part)

    def ag_send_part(q, i, where, axis, k, event):
        part = ag_part(GATHER[q][i], where)
        send(part, part, ag_send, ag_recv.at[q, i, event], along(axis, k))

    def ag_core(q, i, where, plane):
        part = ag_part(GATHER[q][i], where)
        send(part, part, dd_send, dd_recv.at[q, i, plane], device(dc=1))

    def ag_wait(q, i, event, where):
        wait(ag_part(GATHER[q][i], where), ag_recv.at[q, i, event])

    def parts_of(q):
        return [(i,) + ORDERS[part[0]] for i, part in enumerate(GATHER[q])]

    one_line, two_lines, four_lines = {X: 0, Y: 0}, {X: 0, Y: slice(0, 2)}, {X: 0}

    def ag0(q):
        for i, a1, a2, a3 in parts_of(q):
            for k in (1, 3, 2):
                ag_send_part(q, i, {a1: me[a1], a2: me[a2], a3: me[a3]}, a1, k, 0)
            for axis, event in ((a2, 1), (a3, 3)):
                for k in (1, 3):
                    ag_send_part(q, i, {a1: me[a1], a2: me[a2], a3: me[a3]}, axis, k, event)

    def ag1(q):
        for i, a1, a2, a3 in parts_of(q):
            ag_wait(q, i, 0, {X: 0, Y: 0, Z: slice(0, 3)})
            line = {a2: me[a2], a3: me[a3]}
            for j in (1, 3, 2):
                block = {a1: wrap(me[a1] + j), **line}
                for axis, event in ((a2, 1), (a3, 3)):
                    for k in (1, 3):
                        ag_send_part(q, i, block, axis, k, event)

    def ag2(q):
        for i, a1, a2, a3 in parts_of(q):
            m2, m3 = me[a2], me[a3]
            ag_wait(q, i, 1, two_lines)
            left, right = wrap(m2 - 1), wrap(m2 + 1)
            ag_send_part(q, i, {a1: LOW, a2: left, a3: m3}, a2, 1, 2)
            ag_send_part(q, i, {a1: HIGH, a2: right, a3: m3}, a2, 3, 2)
            for j in (left, right):
                for k in (1, 3):
                    ag_send_part(q, i, {a2: j, a3: m3}, a3, k, 4)

    def ag_last(q, i, lines, event, waited):
        a1, a2, a3 = ORDERS[GATHER[q][i][0]]
        left, right = wrap(me[a3] - 1), wrap(me[a3] + 1)
        ag_wait(q, i, event, waited)
        for j in lines:
            ag_send_part(q, i, {a1: LOW, a2: j, a3: left}, a3, 1, event + 3)
            ag_send_part(q, i, {a1: HIGH, a2: j, a3: right}, a3, 3, event + 3)
        for j in lines:
            ag_core(q, i, {a2: j, a3: left}, 1)
            ag_core(q, i, {a2: j, a3: right}, 1)

    def ag3(q):
        for i, a1, a2, a3 in parts_of(q):
            ag_last(q, i, (me[a2],), 3, two_lines)

    def ag4(q):
        for i, a1, a2, a3 in parts_of(q):
            ag_wait(q, i, 2, one_line)
            line = {a2: wrap(me[a2] + 2), a3: me[a3]}
            for k in (1, 3):
                ag_send_part(q, i, line, a3, k, 5)
            ag_core(q, i, {a3: me[a3]}, 0)

    def ag5(q):
        for i, a1, a2, a3 in parts_of(q):
            ag_last(q, i, (wrap(me[a2] - 1), wrap(me[a2] + 1)), 4, four_lines)

    def ag6(q):
        for i, a1, a2, a3 in parts_of(q):
            ag_last(q, i, (wrap(me[a2] + 2),), 5, two_lines)

    def ag7(q):
        for i, a1, a2, a3 in parts_of(q):
            far = wrap(me[a3] + 2)
            ag_wait(q, i, 6, one_line)
            ag_core(q, i, {a2: me[a2], a3: far}, 2)
            ag_wait(q, i, 7, two_lines)
            ag_core(q, i, {a2: wrap(me[a2] - 1), a3: far}, 2)
            ag_core(q, i, {a2: wrap(me[a2] + 1), a3: far}, 2)

    def ag8(q):
        for i, a1, a2, a3 in parts_of(q):
            far = wrap(me[a3] + 2)
            ag_wait(q, i, 8, one_line)
            ag_core(q, i, {a2: wrap(me[a2] + 2), a3: far}, 2)

    def ag_core_wait(q, i, plane):
        planes = pl.ds(0, 2) if plane == 1 else 0
        wait(pick(g, (1 - c,), (X, Y, Z), {X: planes}, GATHER[q][i]), dd_recv.at[q, i, plane])

    def early_core_wait(plane):
        for q in range(ROUNDS):
            ag_core_wait(q, len(GATHER[q]) - 1, plane)

    def late_core_wait():
        for q in range(ROUNDS):
            for i in range(len(GATHER[q]) - 1):
                for plane in range(3):
                    ag_core_wait(q, i, plane)

    def logits(m, core, chips, first, last):
        rows = [g[core, i, :, :, :, m * WIDTH + first:m * WIDTH + last].reshape(T, last - first) for i in chips]
        if m == 0:
            weights = [w[i * 2 + core, :, first:last] for i in chips]
        else:
            weights = [wr[i * 2 + core, :, :, :, first:last].reshape(VW, last - first) for i in chips]
        acc = (lg, rlg)[m]
        acc[...] += lax.dot_general(
            jnp.concatenate(weights, axis=1), jnp.concatenate(rows, axis=1),
            (((1,), (1,)), ((), ())), preferred_element_type=f32,
        )

    def early_logits(core, first, count, stride=1):
        def step(j, carry):
            for m in range(2):
                logits(m, core, (wrap(x + first + stride * j),), EARLY[m], WIDTH)
            return carry

        lax.fori_loop(0, count, step, 0)

    def late_logits(m, core):
        logits(m, core, (0, 1, 2, 3), 0, EARLY[m])

    def clear():
        lg[...] = jnp.zeros((VW, T), f32)
        rlg[...] = jnp.zeros((VW, T), f32)

    def local_stats():
        l, rf = lg[...], rlg[...]
        m = jnp.max(l, axis=0, keepdims=True)
        rm = jnp.max(rf, axis=0, keepdims=True)
        lm, rfm = l - m, rf - rm
        e = jnp.exp(lm)
        mass = jnp.sum(e, axis=0, keepdims=True)
        rmass = jnp.sum(jnp.exp(rfm), axis=0, keepdims=True)
        d = jnp.sum(e * (lm - rfm), axis=0, keepdims=True)
        ln, rln = jnp.log(mass), jnp.log(rmass)
        lse, rlse, kl = two_rows(m + ln), two_rows(rm + rln), two_rows(d / mass - ln + rln)
        st_s[0] = jnp.concatenate([lse, rlse, kl, kl], axis=0)

    def stats_send(phase):
        for i, peer in enumerate(groups[phase]):
            send(
                st_s.at[phase], st_r.at[starts[phase] + i],
                st_send.at[phase], st_recv.at[phase], device(**peer),
            )

    def stats_wait(phase):
        n = len(groups[phase])
        wait(st_r.at[pl.ds(starts[phase], n)], st_recv.at[phase])
        terms = [st_s[phase]] + [st_r[starts[phase] + i] for i in range(n)]
        m = functools.reduce(jnp.maximum, [a[0:2] for a in terms])
        rm = functools.reduce(jnp.maximum, [a[2:4] for a in terms])
        shares = [jnp.exp(a[0:2] - m) for a in terms]
        mass = sum(shares)
        lse = m + jnp.log(mass)
        rlse = rm + jnp.log(sum(jnp.exp(a[2:4] - rm) for a in terms))
        kl = sum(e * (a[4:6] + (a[0:2] - lse) - (a[2:4] - rlse)) for e, a in zip(shares, terms)) / mass
        st_s[phase + 1] = jnp.concatenate([lse, rlse, kl, kl], axis=0)

    def grads():
        a = st_s[2]
        lse, rlse, divergence = one_row(a[0:2]), one_row(a[2:4]), one_row(a[4:6])
        weight = loss_scale * mask_ref[...].astype(f32)
        adv = adv_ref[...]
        place = ids_ref[...] - offset

        def step(i, carry):
            rows = pl.multiple_of(i * 128, 128)
            lp = lg[pl.ds(rows, 128), :] - lse
            rlp = rlg[pl.ds(rows, 128), :] - rlse
            p = jnp.exp(lp)
            entry = rows + lax.broadcasted_iota(jnp.int32, (128, T), 0)
            target = (entry == place).astype(f32)
            value = weight * (adv * (p - target) + penalty_weight * p * (lp - rlp - divergence))
            gv[pl.ds(rows, 128), :] = value.astype(bf16)
            gt[0, :, pl.ds(rows, 128)] = value.T.astype(bf16)
            return carry

        lax.fori_loop(0, VW // 128, step, 0)

    turns = (wrap(x + 2), wrap(x + 1), wrap(x - 1), x)

    def products(k):
        i = turns[k]
        both = jnp.concatenate([gt[0], gt[1]], axis=1)
        rows = jnp.dot(both, jnp.concatenate([w[i * 2 + c], w2[i]], axis=0), preferred_element_type=f32)
        wr[4 + i] = rows.astype(bf16).reshape(4, 4, R, WIDTH)

    def grads_swap():
        send(gt.at[0], gt.at[1], swap_send.at[1], swap_recv.at[1], device(dc=1))

    def grads_swap_wait():
        wait(w2, swap_recv.at[0])
        wait(gt.at[1], swap_recv.at[1])

    def order(r):
        a1, a2, a3 = SUM_ORDERS[r]
        plane = tuple(a for a in (X, Y, Z) if a != a3)
        at = lambda ref, where: pick(ref, (), plane, where, REDUCE[r])
        line = lambda ref, where: pick(ref, (), (a1,), where, REDUCE[r])

        def mine(where):
            where = dict(where)
            j = where.get(X, ALL)
            where[X] = j + 4 if not isinstance(j, slice) else slice(4 + (j.start or 0), 4 + (j.stop or 4))
            return pick(wr, (), (X, Y, Z), where, REDUCE[r])

        return a1, a2, a3, at, line, mine

    def add(place, other):
        place[...] = (place[...].astype(f32) + other[...].astype(f32)).astype(bf16)

    def rs3_start(k):
        i, ss = turns[k], rs_send.at[0]
        for r in (0, 2):
            a1, a2, a3, at, line, mine = order(r)
            for part, step in ((LOW, 1), (HIGH, 3)):
                send(
                    mine({X: i, a3: wrap(me[a3] + 2), a1: part}), at(fw, {X: i, a1: part}),
                    ss, rs3.at[r, 0, k], along(a3, step),
                )
        if k == 0:
            a1, a2, a3, at, line, mine = order(1)
            for part, step in ((LOW, 1), (HIGH, 3)):
                send(mine({X: i, a1: part}), at(fw, {a1: part}), ss, rs3.at[1, 0, 0], along(X, step))

    def rs3_raw(k):
        i, ss = turns[k], rs_send.at[0]
        for r in (0, 2):
            a1, a2, a3, at, line, mine = order(r)
            for part, step, dst in ((HIGH, 1, rl), (LOW, 3, rr)):
                send(
                    mine({X: i, a3: wrap(me[a3] + step), a1: part}), at(dst, {X: i, a1: part}),
                    ss, rs3.at[r, 1, k], along(a3, step),
                )
        if k in (1, 2):
            a1, a2, a3, at, line, mine = order(1)
            part, step, dst = ((HIGH, 1, rl), (LOW, 3, rr))[k - 1]
            send(mine({X: i, a1: part}), at(dst, {a1: part}), ss, rs3.at[1, 1, 0], along(X, step))

    def rs3_middle(k):
        i, ss = turns[k], rs_send.at[0]
        for r in (0, 2):
            a1, a2, a3, at, line, mine = order(r)
            wait(at(fw, {X: i}), rs3.at[r, 0, k])
            for part, step, dst in ((LOW, 1, rl), (HIGH, 3, rr)):
                place = at(fw, {X: i, a1: part})
                add(place, mine({X: i, a3: wrap(me[a3] + step), a1: part}))
                send(place, at(dst, {X: i, a1: part}), ss, rs3.at[r, 2, k], along(a3, step))

    def rs3_middle_x():
        a1, a2, a3, at, line, mine = order(1)
        wait(at(fw, {}), rs3.at[1, 0, 0])
        for part, to, step, dst in ((LOW, turns[1], 1, rl), (HIGH, turns[2], 3, rr)):
            place = at(fw, {a1: part})
            add(place, mine({X: to, a1: part}))
            send(place, at(dst, {a1: part}), rs_send.at[0], rs3.at[1, 2, 0], along(X, step))

    def summed(at, where, own):
        total = own[...].astype(f32) + at(rl, where)[...].astype(f32) + at(rr, where)[...].astype(f32)
        at(t3, where)[...] = total.astype(bf16)

    def rs3_end_lines(k):
        i, ss = turns[k], rs_send.at[1]
        for r in (0, 2):
            a1, a2, a3, at, line, mine = order(r)
            wait(at(rl, {X: i}), rs3.at[r, 1, k])
            wait(at(rr, {X: i}), rs3.at[r, 2, k])
            summed(at, {X: i}, mine({X: i, a3: me[a3]}))
            if k == 0:
                send(at(t3, {X: i, a1: LOW}), line(fw2, {a1: LOW}), ss, rs2.at[r, 0], along(X, 1))
                send(at(t3, {X: i, a1: HIGH}), line(fw2, {a1: HIGH}), ss, rs2.at[r, 0], along(X, 3))
            elif k == 1:
                send(at(t3, {X: i, a1: HIGH}), line(rl2, {a1: HIGH}), ss, rs2.at[r, 1], along(X, 1))
            elif k == 2:
                send(at(t3, {X: i, a1: LOW}), line(rr2, {a1: LOW}), ss, rs2.at[r, 1], along(X, 3))

    def rs3_end(r):
        ss = rs_send.at[1]
        a1, a2, a3, at, line, mine = order(r)
        wait(at(rl, {}), rs3.at[r, 1, 0])
        wait(at(rr, {}), rs3.at[r, 2, 0])
        summed(at, {}, mine({a3: me[a3]}))
        far, right, left = wrap(me[a2] + 2), wrap(me[a2] + 1), wrap(me[a2] - 1)
        send(at(t3, {a1: LOW, a2: far}), line(fw2, {a1: LOW}), ss, rs2.at[r, 0], along(a2, 1))
        send(at(t3, {a1: HIGH, a2: far}), line(fw2, {a1: HIGH}), ss, rs2.at[r, 0], along(a2, 3))
        send(at(t3, {a1: HIGH, a2: right}), line(rl2, {a1: HIGH}), ss, rs2.at[r, 1], along(a2, 1))
        send(at(t3, {a1: LOW, a2: left}), line(rr2, {a1: LOW}), ss, rs2.at[r, 1], along(a2, 3))

    def rs2_middle(r):
        a1, a2, a3, at, line, mine = order(r)
        wait(line(fw2, {}), rs2.at[r, 0])
        for part, to, step, dst in ((LOW, wrap(me[a2] + 1), 1, rl2), (HIGH, wrap(me[a2] - 1), 3, rr2)):
            place = line(fw2, {a1: part})
            add(place, at(t3, {a1: part, a2: to}))
            send(place, line(dst, {a1: part}), rs_send.at[1], rs2.at[r, 2], along(a2, step))

    def rs2_end(r):
        a1, a2, a3, at, line, mine = order(r)
        wait(line(rl2, {}), rs2.at[r, 1])
        wait(line(rr2, {}), rs2.at[r, 2])
        total = at(t3, {a2: me[a2]})[...].astype(f32) + line(rl2, {})[...].astype(f32)
        line(t2, {})[...] = total + line(rr2, {})[...].astype(f32)
        for k in (1, 2, 3):
            send(
                line(t2, {a1: wrap(me[a1] + k)}), line(r1, {a1: k - 1}), rs_send.at[2], rs1.at[r], along(a1, k)
            )

    def rs1_end(r):
        a1, a2, a3, at, line, mine = order(r)
        _, row, rows, col, cols = REDUCE[r]
        wait(line(r1, {}), rs1.at[r])
        total = line(t2, {a1: me[a1]})[...]
        for k in range(3):
            total += line(r1, {a1: k})[...]
        out_h[row:row + rows, col:col + cols] = total

    def head(first, last):
        def step(i, carry):
            rows = g[lax.rem(i, 2), i // 2, :, :, :, 0:WIDTH].reshape(T, WIDTH)
            total = jnp.dot(gv[...], rows, preferred_element_type=f32)
            out_w[:, pl.ds(pl.multiple_of(i * WIDTH, WIDTH), WIDTH)] = total.astype(bf16)
            return carry

        lax.fori_loop(first, last, step, 0)

    def weights_wait(m):
        ref = (w, wr)[m]
        wait(ref, load_sem.at[2 + m])

    def drain():
        wait(out_w.at[:, pl.ds(0, 63 * 128)], ag_send)
        wait(g.at[c], dd_send)
        for phase in range(2):
            n = len(groups[phase])
            wait(st_r.at[pl.ds(starts[phase], n)], st_send.at[phase])
        wait(w2, swap_send.at[0])
        wait(gt.at[0], swap_send.at[1])
        wait(wr.at[pl.ds(0, 3)], rs_send.at[0])
        wait(wr.at[0, pl.ds(0, 3)], rs_send.at[1])
        wait(t2.at[pl.ds(0, 3)], rs_send.at[2])

    ag0(0)
    ag0(1)
    weights_start()
    clear()
    for step in (ag1, ag2, ag3, ag4):
        step(0)
        step(1)
    weights_wait(0)
    weights_wait(1)
    early_logits(c, 0, 1)
    ag5(0)
    ag5(1)
    early_core_wait(0)
    early_logits(1 - c, 0, 1)
    ag6(0)
    ag6(1)
    early_logits(c, 1, 2, 2)
    ag7(0)
    ag7(1)
    early_core_wait(1)
    early_logits(1 - c, 1, 2, 2)
    ag8(0)
    late_logits(0, c)
    ag8(1)
    late_logits(1, c)
    early_logits(c, 2, 1)
    early_core_wait(2)
    early_logits(1 - c, 2, 1)
    late_core_wait()
    late_logits(0, 1 - c)
    late_logits(1, 1 - c)
    local_stats()
    stats_send(0)
    stats_wait(0)
    stats_send(1)
    stats_wait(1)
    grads()
    grads_swap()
    head(0, 2)
    grads_swap_wait()
    products(0)
    rs3_start(0)
    products(1)
    rs3_start(1)
    products(2)
    rs3_start(2)
    rs3_raw(0)
    rs3_middle(0)
    rs3_raw(1)
    products(3)
    rs3_start(3)
    rs3_middle(1)
    rs3_raw(2)
    rs3_middle_x()
    rs3_middle(2)
    rs3_raw(3)
    head(2, 3)
    rs3_middle(3)
    rs3_end_lines(0)
    head(3, 4)
    rs3_end(1)
    rs3_end_lines(1)
    rs3_end_lines(2)
    rs2_middle(0)
    rs2_middle(2)
    rs2_middle(1)
    head(4, 6)
    rs3_end_lines(3)
    rs2_end(0)
    rs2_end(2)
    rs2_end(1)
    head(6, 8)
    rs1_end(0)
    rs1_end(2)
    rs1_end(1)
    drain()


def shards(hidden, ref_hidden, w_policy, w_ref, token_ids, loss_mask, advantages):
    any_space = pl.BlockSpec(memory_space=pl.ANY)
    vmem = pl.BlockSpec(memory_space=pltpu.VMEM)
    dma = pltpu.SemaphoreType.DMA
    return pl.pallas_call(
        kernel,
        out_shape=(
            pltpu.VMEM((R, WIDTH), f32),
            pltpu.VMEM((VW, 8 * WIDTH), bf16),
        ),
        in_specs=[any_space] * 4 + [vmem] * 3,
        out_specs=(vmem, vmem),
        scratch_shapes=[
            pltpu.VMEM((2, 4, 4, 4, R, 2 * WIDTH), bf16),
            pltpu.VMEM((8, VW, WIDTH), bf16),
            pltpu.VMEM((8, 4, 4, R, WIDTH), bf16),
            pltpu.VMEM((4, VW, WIDTH), bf16),
            pltpu.VMEM((VW, T), f32),
            pltpu.VMEM((VW, T), f32),
            pltpu.VMEM((VW, T), bf16),
            pltpu.VMEM((2, T, VW), bf16),
            pltpu.VMEM((3, 8, T // 2), f32),
            pltpu.VMEM((22, 8, T // 2), f32),
            pltpu.VMEM((4, 4, R, WIDTH), bf16),
            pltpu.VMEM((4, 4, R, WIDTH), bf16),
            pltpu.VMEM((4, 4, R, WIDTH), bf16),
            pltpu.VMEM((4, 4, R, WIDTH), bf16),
            pltpu.VMEM((4, R, WIDTH), bf16),
            pltpu.VMEM((4, R, WIDTH), bf16),
            pltpu.VMEM((4, R, WIDTH), bf16),
            pltpu.VMEM((4, R, WIDTH), f32),
            pltpu.VMEM((3, R, WIDTH), f32),
            dma((4,)),
            dma,
            dma((ROUNDS, PARTS, 9)),
            dma,
            dma((ROUNDS, PARTS, 3)),
            dma((2,)),
            dma((2,)),
            dma((2,)),
            dma((2,)),
            dma((3,)),
            dma((3, 3, 4)),
            dma((3, 3)),
            dma((3,)),
        ],
        compiler_params=pltpu.CompilerParams(
            collective_id=0, has_side_effects=True, vmem_limit_bytes=50 * 2**20
        ),
        cost_estimate=pl.CostEstimate(flops=4 * 2 * 512 * 512 * 8192, bytes_accessed=3 * 2**23, transcendentals=2**20),
        name="head_step",
    )(
        hidden, ref_hidden, w_policy, w_ref.reshape(4, 4, R, 8 * WIDTH),
        token_ids.reshape(1, T), loss_mask.reshape(1, T), advantages.reshape(1, T),
    )


def solution(mesh):
    placed = (
        P("section", "tensor"),
        P("section", "tensor"),
        P(("section", "tensor"), None),
        P(("section", "tensor"), None),
        P(),
        P(),
        P(),
    )
    return jax.shard_map(
        shards,
        mesh=mesh,
        in_specs=placed,
        out_specs=(P("section", "tensor"), P(("section", "tensor"), None)),
        check_vma=False,
    )
```

```python
import functools

import jax
import jax.numpy as jnp
from jax import lax
from jax.experimental import pallas as pl
from jax.experimental.pallas import tpu as pltpu
from jax.sharding import PartitionSpec as P

MESH = pl.DeviceIdType.MESH
bf16, f32 = jnp.bfloat16, jnp.float32

loss_scale = 4.0
penalty_weight = 0.2

R = 32
WIDTH = 1024
T = 16 * R
VW = 512
X, Y, Z = 0, 1, 2
ORDERS = ((X, Y, Z), (Y, Z, X), (Z, X, Y))
SUM_ORDERS = ((Y, X, Z), (Z, Y, X), (Z, X, Y))
GATHER = (
    ((0, 0, 32, 0, 384), (2, 0, 32, 384, 384), (1, 0, 32, 768, 256)),
    ((0, 0, 32, 1024, 256), (2, 0, 32, 1280, 256), (0, 0, 16, 1536, 128), (2, 16, 16, 1536, 128), (1, 0, 32, 1664, 384)),
)
EARLY = (768, 640)
REDUCE = ((0, 0, 32, 0, 384), (1, 0, 32, 384, 256), (2, 0, 32, 640, 384))
ROUNDS, PARTS = 2, 5
ALL = slice(None)
LOW, HIGH = slice(0, 2), slice(2, 4)


def wrap(i):
    return lax.rem(i + 4, 4)


def two_rows(a):
    return jnp.concatenate([a[:, :T // 2], a[:, T // 2:]], axis=0)


def one_row(a):
    return jnp.concatenate([a[0:1], a[1:2]], axis=1)


def pick(ref, lead, axes, where, part):
    index = tuple(lead)
    for axis in axes:
        index += (where.get(axis, ALL),)
    return ref.at[index + (pl.ds(part[1], part[2]), pl.ds(part[3], part[4]))]


def kernel(
    hid, rhid, w_hbm, wr_hbm, ids_ref, mask_ref, adv_ref, out_h, out_w,
    g, w, wr, w2, lg, rlg, gv, gt, st_s, st_r,
    fw, rl, rr, t3, fw2, rl2, rr2, t2, r1,
    load_sem, ag_send, ag_recv, dd_send, dd_recv, st_send, st_recv,
    swap_send, swap_recv, rs_send, rs3, rs2, rs1,
):
    section, tensor = lax.axis_index("section"), lax.axis_index("tensor")
    x, c = tensor // 2, lax.rem(tensor, 2)
    y, z = section // 4, lax.rem(section, 4)
    me = (x, y, z)
    offset = (section * 8 + tensor) * VW

    def device(dx=0, dy=0, dz=0, dc=0):
        return (
            lax.rem(y + dy + 4, 4) * 4 + lax.rem(z + dz + 4, 4),
            lax.rem(x + dx + 4, 4) * 2 + lax.rem(c + dc, 2),
        )

    def along(axis, k):
        step = [0, 0, 0]
        step[axis] = k
        return device(*step)

    def send(src, dst, ssem, rsem, to):
        pltpu.make_async_remote_copy(
            src_ref=src, dst_ref=dst, send_sem=ssem, recv_sem=rsem, device_id=to, device_id_type=MESH
        ).start()

    def wait(ref, sem):
        pltpu.make_async_copy(ref, ref, sem).wait()

    tensor_peers = [(kx, kc) for kx in range(4) for kc in range(2) if (kx, kc) != (0, 0)]
    groups = (
        [dict(dx=kx, dc=kc) for kx, kc in tensor_peers],
        [dict(dy=ky, dz=kz) for ky in range(4) for kz in range(4) if (ky, kz) != (0, 0)],
    )
    starts = (0, 7)
    peers = [peer for group in groups for peer in group]

    loads = [
        pltpu.make_async_copy(src, g.at[c, x, y, z, :, pl.ds(m * WIDTH, WIDTH)], load_sem.at[m])
        for m, src in enumerate((hid, rhid))
    ]
    for copy in loads:
        copy.start()
    barrier = pltpu.get_barrier_semaphore()
    for peer in peers:
        pl.semaphore_signal(barrier, inc=1, device_id=device(**peer), device_id_type=MESH)
    for copy in loads:
        copy.wait()
    pl.semaphore_wait(barrier, len(peers))

    def weights_start():
        for i in range(8):
            cols = pl.ds(i * WIDTH, WIDTH)
            pltpu.make_async_copy(w_hbm.at[:, cols], w.at[i], load_sem.at[2]).start()
        for i in range(8):
            cols = pl.ds(i * WIDTH, WIDTH)
            pltpu.make_async_copy(wr_hbm.at[:, :, :, cols], wr.at[i], load_sem.at[3]).start()
        for i in range(4):
            cols = pl.ds(pl.multiple_of((i * 2 + 1 - c) * WIDTH, WIDTH), WIDTH)
            send(w_hbm.at[:, cols], w2.at[i], swap_send.at[0], swap_recv.at[0], device(dc=1))

    def ag_part(part, where):
        return pick(g, (c,), (X, Y, Z), where, part)

    def ag_send_part(q, i, where, axis, k, event):
        part = ag_part(GATHER[q][i], where)
        send(part, part, ag_send, ag_recv.at[q, i, event], along(axis, k))

    def ag_core(q, i, where, plane):
        part = ag_part(GATHER[q][i], where)
        send(part, part, dd_send, dd_recv.at[q, i, plane], device(dc=1))

    def ag_wait(q, i, event, where):
        wait(ag_part(GATHER[q][i], where), ag_recv.at[q, i, event])

    def parts_of(q):
        return [(i,) + ORDERS[part[0]] for i, part in enumerate(GATHER[q])]

    one_line, two_lines, four_lines = {X: 0, Y: 0}, {X: 0, Y: slice(0, 2)}, {X: 0}

    def ag0(q):
        for i, a1, a2, a3 in parts_of(q):
            for k in (1, 3, 2):
                ag_send_part(q, i, {a1: me[a1], a2: me[a2], a3: me[a3]}, a1, k, 0)
            for axis, event in ((a2, 1), (a3, 3)):
                for k in (1, 3):
                    ag_send_part(q, i, {a1: me[a1], a2: me[a2], a3: me[a3]}, axis, k, event)

    def ag1(q):
        for i, a1, a2, a3 in parts_of(q):
            ag_wait(q, i, 0, {X: 0, Y: 0, Z: slice(0, 3)})
            line = {a2: me[a2], a3: me[a3]}
            for j in (1, 3, 2):
                block = {a1: wrap(me[a1] + j), **line}
                for axis, event in ((a2, 1), (a3, 3)):
                    for k in (1, 3):
                        ag_send_part(q, i, block, axis, k, event)

    def ag2(q):
        for i, a1, a2, a3 in parts_of(q):
            m2, m3 = me[a2], me[a3]
            ag_wait(q, i, 1, two_lines)
            left, right = wrap(m2 - 1), wrap(m2 + 1)
            ag_send_part(q, i, {a1: LOW, a2: left, a3: m3}, a2, 1, 2)
            ag_send_part(q, i, {a1: HIGH, a2: right, a3: m3}, a2, 3, 2)
            for j in (left, right):
                for k in (1, 3):
                    ag_send_part(q, i, {a2: j, a3: m3}, a3, k, 4)

    def ag_last(q, i, lines, event, waited):
        a1, a2, a3 = ORDERS[GATHER[q][i][0]]
        left, right = wrap(me[a3] - 1), wrap(me[a3] + 1)
        ag_wait(q, i, event, waited)
        for j in lines:
            ag_send_part(q, i, {a1: LOW, a2: j, a3: left}, a3, 1, event + 3)
            ag_send_part(q, i, {a1: HIGH, a2: j, a3: right}, a3, 3, event + 3)
        for j in lines:
            ag_core(q, i, {a2: j, a3: left}, 1)
            ag_core(q, i, {a2: j, a3: right}, 1)

    def ag3(q):
        for i, a1, a2, a3 in parts_of(q):
            ag_last(q, i, (me[a2],), 3, two_lines)

    def ag4(q):
        for i, a1, a2, a3 in parts_of(q):
            ag_wait(q, i, 2, one_line)
            line = {a2: wrap(me[a2] + 2), a3: me[a3]}
            for k in (1, 3):
                ag_send_part(q, i, line, a3, k, 5)
            ag_core(q, i, {a3: me[a3]}, 0)

    def ag5(q):
        for i, a1, a2, a3 in parts_of(q):
            ag_last(q, i, (wrap(me[a2] - 1), wrap(me[a2] + 1)), 4, four_lines)

    def ag6(q):
        for i, a1, a2, a3 in parts_of(q):
            ag_last(q, i, (wrap(me[a2] + 2),), 5, two_lines)

    def ag7(q):
        for i, a1, a2, a3 in parts_of(q):
            far = wrap(me[a3] + 2)
            ag_wait(q, i, 6, one_line)
            ag_core(q, i, {a2: me[a2], a3: far}, 2)
            ag_wait(q, i, 7, two_lines)
            ag_core(q, i, {a2: wrap(me[a2] - 1), a3: far}, 2)
            ag_core(q, i, {a2: wrap(me[a2] + 1), a3: far}, 2)

    def ag8(q):
        for i, a1, a2, a3 in parts_of(q):
            far = wrap(me[a3] + 2)
            ag_wait(q, i, 8, one_line)
            ag_core(q, i, {a2: wrap(me[a2] + 2), a3: far}, 2)

    def ag_core_wait(q, i, plane):
        planes = pl.ds(0, 2) if plane == 1 else 0
        wait(pick(g, (1 - c,), (X, Y, Z), {X: planes}, GATHER[q][i]), dd_recv.at[q, i, plane])

    def early_core_wait(plane):
        for q in range(ROUNDS):
            ag_core_wait(q, len(GATHER[q]) - 1, plane)

    def late_core_wait():
        for q in range(ROUNDS):
            for i in range(len(GATHER[q]) - 1):
                for plane in range(3):
                    ag_core_wait(q, i, plane)

    def logits(m, core, chips, first, last):
        rows = [g[core, i, :, :, :, m * WIDTH + first:m * WIDTH + last].reshape(T, last - first) for i in chips]
        if m == 0:
            weights = [w[i * 2 + core, :, first:last] for i in chips]
        else:
            weights = [wr[i * 2 + core, :, :, :, first:last].reshape(VW, last - first) for i in chips]
        acc = (lg, rlg)[m]
        acc[...] += lax.dot_general(
            jnp.concatenate(weights, axis=1), jnp.concatenate(rows, axis=1),
            (((1,), (1,)), ((), ())), preferred_element_type=f32,
        )

    def early_logits(core, first, count, stride=1):
        def step(j, carry):
            for m in range(2):
                logits(m, core, (wrap(x + first + stride * j),), EARLY[m], WIDTH)
            return carry

        lax.fori_loop(0, count, step, 0)

    def late_logits(m, core):
        logits(m, core, (0, 1, 2, 3), 0, EARLY[m])

    def clear():
        lg[...] = jnp.zeros((VW, T), f32)
        rlg[...] = jnp.zeros((VW, T), f32)

    def local_stats():
        l, rf = lg[...], rlg[...]
        m = jnp.max(l, axis=0, keepdims=True)
        rm = jnp.max(rf, axis=0, keepdims=True)
        lm, rfm = l - m, rf - rm
        e = jnp.exp(lm)
        mass = jnp.sum(e, axis=0, keepdims=True)
        rmass = jnp.sum(jnp.exp(rfm), axis=0, keepdims=True)
        d = jnp.sum(e * (lm - rfm), axis=0, keepdims=True)
        ln, rln = jnp.log(mass), jnp.log(rmass)
        lse, rlse, kl = two_rows(m + ln), two_rows(rm + rln), two_rows(d / mass - ln + rln)
        st_s[0] = jnp.concatenate([lse, rlse, kl, kl], axis=0)

    def stats_send(phase):
        for i, peer in enumerate(groups[phase]):
            send(
                st_s.at[phase], st_r.at[starts[phase] + i],
                st_send.at[phase], st_recv.at[phase], device(**peer),
            )

    def stats_wait(phase):
        n = len(groups[phase])
        wait(st_r.at[pl.ds(starts[phase], n)], st_recv.at[phase])
        terms = [st_s[phase]] + [st_r[starts[phase] + i] for i in range(n)]
        m = functools.reduce(jnp.maximum, [a[0:2] for a in terms])
        rm = functools.reduce(jnp.maximum, [a[2:4] for a in terms])
        shares = [jnp.exp(a[0:2] - m) for a in terms]
        mass = sum(shares)
        lse = m + jnp.log(mass)
        rlse = rm + jnp.log(sum(jnp.exp(a[2:4] - rm) for a in terms))
        kl = sum(e * (a[4:6] + (a[0:2] - lse) - (a[2:4] - rlse)) for e, a in zip(shares, terms)) / mass
        st_s[phase + 1] = jnp.concatenate([lse, rlse, kl, kl], axis=0)

    def grads():
        a = st_s[2]
        lse, rlse, divergence = one_row(a[0:2]), one_row(a[2:4]), one_row(a[4:6])
        weight = loss_scale * mask_ref[...].astype(f32)
        adv = adv_ref[...]
        place = ids_ref[...] - offset

        def step(i, carry):
            rows = pl.multiple_of(i * 128, 128)
            lp = lg[pl.ds(rows, 128), :] - lse
            rlp = rlg[pl.ds(rows, 128), :] - rlse
            p = jnp.exp(lp)
            entry = rows + lax.broadcasted_iota(jnp.int32, (128, T), 0)
            target = (entry == place).astype(f32)
            value = weight * (adv * (p - target) + penalty_weight * p * (lp - rlp - divergence))
            gv[pl.ds(rows, 128), :] = value.astype(bf16)
            gt[0, :, pl.ds(rows, 128)] = value.T.astype(bf16)
            part = pl.ds(rows, 128)
            send(gt.at[0, :, part], gt.at[1, :, part], swap_send.at[1], swap_recv.at[1], device(dc=1))
            return carry

        lax.fori_loop(0, VW // 128, step, 0)

    turns = (wrap(x + 2), wrap(x + 1), wrap(x - 1), x)

    def products(k):
        i = turns[k]
        both = jnp.concatenate([gt[0], gt[1]], axis=1)
        rows = jnp.dot(both, jnp.concatenate([w[i * 2 + c], w2[i]], axis=0), preferred_element_type=f32)
        wr[4 + i] = rows.astype(bf16).reshape(4, 4, R, WIDTH)

    def grads_swap_wait():
        wait(w2, swap_recv.at[0])
        wait(gt.at[1], swap_recv.at[1])

    def order(r):
        a1, a2, a3 = SUM_ORDERS[r]
        plane = tuple(a for a in (X, Y, Z) if a != a3)
        at = lambda ref, where: pick(ref, (), plane, where, REDUCE[r])
        line = lambda ref, where: pick(ref, (), (a1,), where, REDUCE[r])

        def mine(where):
            where = dict(where)
            j = where.get(X, ALL)
            where[X] = j + 4 if not isinstance(j, slice) else slice(4 + (j.start or 0), 4 + (j.stop or 4))
            return pick(wr, (), (X, Y, Z), where, REDUCE[r])

        return a1, a2, a3, at, line, mine

    def add(place, other):
        place[...] = (place[...].astype(f32) + other[...].astype(f32)).astype(bf16)

    def rs3_start(k):
        i, ss = turns[k], rs_send.at[0]
        for r in (0, 2):
            a1, a2, a3, at, line, mine = order(r)
            for part, step in ((LOW, 1), (HIGH, 3)):
                send(
                    mine({X: i, a3: wrap(me[a3] + 2), a1: part}), at(fw, {X: i, a1: part}),
                    ss, rs3.at[r, 0, k], along(a3, step),
                )
        if k == 0:
            a1, a2, a3, at, line, mine = order(1)
            for part, step in ((LOW, 1), (HIGH, 3)):
                send(mine({X: i, a1: part}), at(fw, {a1: part}), ss, rs3.at[1, 0, 0], along(X, step))

    def rs3_raw(k):
        i, ss = turns[k], rs_send.at[0]
        for r in (0, 2):
            a1, a2, a3, at, line, mine = order(r)
            for part, step, dst in ((HIGH, 1, rl), (LOW, 3, rr)):
                send(
                    mine({X: i, a3: wrap(me[a3] + step), a1: part}), at(dst, {X: i, a1: part}),
                    ss, rs3.at[r, 1, k], along(a3, step),
                )
        if k in (1, 2):
            a1, a2, a3, at, line, mine = order(1)
            part, step, dst = ((HIGH, 1, rl), (LOW, 3, rr))[k - 1]
            send(mine({X: i, a1: part}), at(dst, {a1: part}), ss, rs3.at[1, 1, 0], along(X, step))

    def rs3_middle(k):
        i, ss = turns[k], rs_send.at[0]
        for r in (0, 2):
            a1, a2, a3, at, line, mine = order(r)
            wait(at(fw, {X: i}), rs3.at[r, 0, k])
            for part, step, dst in ((LOW, 1, rl), (HIGH, 3, rr)):
                place = at(fw, {X: i, a1: part})
                add(place, mine({X: i, a3: wrap(me[a3] + step), a1: part}))
                send(place, at(dst, {X: i, a1: part}), ss, rs3.at[r, 2, k], along(a3, step))

    def rs3_middle_x():
        a1, a2, a3, at, line, mine = order(1)
        wait(at(fw, {}), rs3.at[1, 0, 0])
        for part, to, step, dst in ((LOW, turns[1], 1, rl), (HIGH, turns[2], 3, rr)):
            place = at(fw, {a1: part})
            add(place, mine({X: to, a1: part}))
            send(place, at(dst, {a1: part}), rs_send.at[0], rs3.at[1, 2, 0], along(X, step))

    def summed(at, where, own):
        total = own[...].astype(f32) + at(rl, where)[...].astype(f32) + at(rr, where)[...].astype(f32)
        at(t3, where)[...] = total.astype(bf16)

    def rs3_end_lines(k):
        i, ss = turns[k], rs_send.at[1]
        for r in (0, 2):
            a1, a2, a3, at, line, mine = order(r)
            wait(at(rl, {X: i}), rs3.at[r, 1, k])
            wait(at(rr, {X: i}), rs3.at[r, 2, k])
            summed(at, {X: i}, mine({X: i, a3: me[a3]}))
            if k == 0:
                send(at(t3, {X: i, a1: LOW}), line(fw2, {a1: LOW}), ss, rs2.at[r, 0], along(X, 1))
                send(at(t3, {X: i, a1: HIGH}), line(fw2, {a1: HIGH}), ss, rs2.at[r, 0], along(X, 3))
            elif k == 1:
                send(at(t3, {X: i, a1: HIGH}), line(rl2, {a1: HIGH}), ss, rs2.at[r, 1], along(X, 1))
            elif k == 2:
                send(at(t3, {X: i, a1: LOW}), line(rr2, {a1: LOW}), ss, rs2.at[r, 1], along(X, 3))

    def rs3_end(r):
        ss = rs_send.at[1]
        a1, a2, a3, at, line, mine = order(r)
        wait(at(rl, {}), rs3.at[r, 1, 0])
        wait(at(rr, {}), rs3.at[r, 2, 0])
        summed(at, {}, mine({a3: me[a3]}))
        far, right, left = wrap(me[a2] + 2), wrap(me[a2] + 1), wrap(me[a2] - 1)
        send(at(t3, {a1: LOW, a2: far}), line(fw2, {a1: LOW}), ss, rs2.at[r, 0], along(a2, 1))
        send(at(t3, {a1: HIGH, a2: far}), line(fw2, {a1: HIGH}), ss, rs2.at[r, 0], along(a2, 3))
        send(at(t3, {a1: HIGH, a2: right}), line(rl2, {a1: HIGH}), ss, rs2.at[r, 1], along(a2, 1))
        send(at(t3, {a1: LOW, a2: left}), line(rr2, {a1: LOW}), ss, rs2.at[r, 1], along(a2, 3))

    def rs2_middle(r):
        a1, a2, a3, at, line, mine = order(r)
        wait(line(fw2, {}), rs2.at[r, 0])
        for part, to, step, dst in ((LOW, wrap(me[a2] + 1), 1, rl2), (HIGH, wrap(me[a2] - 1), 3, rr2)):
            place = line(fw2, {a1: part})
            add(place, at(t3, {a1: part, a2: to}))
            send(place, line(dst, {a1: part}), rs_send.at[1], rs2.at[r, 2], along(a2, step))

    def rs2_end(r):
        a1, a2, a3, at, line, mine = order(r)
        wait(line(rl2, {}), rs2.at[r, 1])
        wait(line(rr2, {}), rs2.at[r, 2])
        total = at(t3, {a2: me[a2]})[...].astype(f32) + line(rl2, {})[...].astype(f32)
        line(t2, {})[...] = total + line(rr2, {})[...].astype(f32)
        for k in (1, 2, 3):
            send(
                line(t2, {a1: wrap(me[a1] + k)}), line(r1, {a1: k - 1}), rs_send.at[2], rs1.at[r], along(a1, k)
            )

    def rs1_end(r):
        a1, a2, a3, at, line, mine = order(r)
        _, row, rows, col, cols = REDUCE[r]
        wait(line(r1, {}), rs1.at[r])
        total = line(t2, {a1: me[a1]})[...]
        for k in range(3):
            total += line(r1, {a1: k})[...]
        out_h[row:row + rows, col:col + cols] = total

    def head(first, last):
        def step(i, carry):
            rows = g[lax.rem(i, 2), i // 2, :, :, :, 0:WIDTH].reshape(T, WIDTH)
            total = jnp.dot(gv[...], rows, preferred_element_type=f32)
            out_w[:, pl.ds(pl.multiple_of(i * WIDTH, WIDTH), WIDTH)] = total.astype(bf16)
            return carry

        lax.fori_loop(first, last, step, 0)

    def weights_wait(m):
        ref = (w, wr)[m]
        wait(ref, load_sem.at[2 + m])

    def drain():
        wait(out_w.at[:, pl.ds(0, 63 * 128)], ag_send)
        wait(g.at[c], dd_send)
        for phase in range(2):
            n = len(groups[phase])
            wait(st_r.at[pl.ds(starts[phase], n)], st_send.at[phase])
        wait(w2, swap_send.at[0])
        wait(gt.at[0], swap_send.at[1])
        wait(wr.at[pl.ds(0, 3)], rs_send.at[0])
        wait(wr.at[0, pl.ds(0, 3)], rs_send.at[1])
        wait(t2.at[pl.ds(0, 3)], rs_send.at[2])

    ag0(0)
    ag0(1)
    weights_start()
    clear()
    for step in (ag1, ag2, ag3, ag4):
        step(0)
        step(1)
    weights_wait(0)
    weights_wait(1)
    early_logits(c, 0, 1)
    ag5(0)
    ag5(1)
    early_core_wait(0)
    early_logits(1 - c, 0, 1)
    ag6(0)
    ag6(1)
    early_logits(c, 1, 2, 2)
    ag7(0)
    ag7(1)
    early_core_wait(1)
    early_logits(1 - c, 1, 2, 2)
    ag8(0)
    late_logits(0, c)
    ag8(1)
    late_logits(1, c)
    early_logits(c, 2, 1)
    early_core_wait(2)
    early_logits(1 - c, 2, 1)
    late_core_wait()
    late_logits(0, 1 - c)
    late_logits(1, 1 - c)
    local_stats()
    stats_send(0)
    stats_wait(0)
    stats_send(1)
    stats_wait(1)
    grads()
    head(0, 1)
    grads_swap_wait()
    products(0)
    rs3_start(0)
    products(1)
    rs3_start(1)
    products(2)
    rs3_start(2)
    rs3_raw(0)
    rs3_middle(0)
    rs3_raw(1)
    products(3)
    rs3_start(3)
    rs3_middle(1)
    rs3_raw(2)
    rs3_middle_x()
    rs3_middle(2)
    rs3_raw(3)
    head(1, 3)
    rs3_middle(3)
    rs3_end_lines(0)
    head(3, 4)
    rs3_end(1)
    rs3_end_lines(1)
    rs3_end_lines(2)
    rs2_middle(0)
    rs2_middle(2)
    rs2_middle(1)
    head(4, 6)
    rs3_end_lines(3)
    rs2_end(0)
    rs2_end(2)
    rs2_end(1)
    head(6, 8)
    rs1_end(0)
    rs1_end(2)
    rs1_end(1)
    drain()


def shards(hidden, ref_hidden, w_policy, w_ref, token_ids, loss_mask, advantages):
    any_space = pl.BlockSpec(memory_space=pl.ANY)
    vmem = pl.BlockSpec(memory_space=pltpu.VMEM)
    dma = pltpu.SemaphoreType.DMA
    return pl.pallas_call(
        kernel,
        out_shape=(
            pltpu.VMEM((R, WIDTH), f32),
            pltpu.VMEM((VW, 8 * WIDTH), bf16),
        ),
        in_specs=[any_space] * 4 + [vmem] * 3,
        out_specs=(vmem, vmem),
        scratch_shapes=[
            pltpu.VMEM((2, 4, 4, 4, R, 2 * WIDTH), bf16),
            pltpu.VMEM((8, VW, WIDTH), bf16),
            pltpu.VMEM((8, 4, 4, R, WIDTH), bf16),
            pltpu.VMEM((4, VW, WIDTH), bf16),
            pltpu.VMEM((VW, T), f32),
            pltpu.VMEM((VW, T), f32),
            pltpu.VMEM((VW, T), bf16),
            pltpu.VMEM((2, T, VW), bf16),
            pltpu.VMEM((3, 8, T // 2), f32),
            pltpu.VMEM((22, 8, T // 2), f32),
            pltpu.VMEM((4, 4, R, WIDTH), bf16),
            pltpu.VMEM((4, 4, R, WIDTH), bf16),
            pltpu.VMEM((4, 4, R, WIDTH), bf16),
            pltpu.VMEM((4, 4, R, WIDTH), bf16),
            pltpu.VMEM((4, R, WIDTH), bf16),
            pltpu.VMEM((4, R, WIDTH), bf16),
            pltpu.VMEM((4, R, WIDTH), bf16),
            pltpu.VMEM((4, R, WIDTH), f32),
            pltpu.VMEM((3, R, WIDTH), f32),
            dma((4,)),
            dma,
            dma((ROUNDS, PARTS, 9)),
            dma,
            dma((ROUNDS, PARTS, 3)),
            dma((2,)),
            dma((2,)),
            dma((2,)),
            dma((2,)),
            dma((3,)),
            dma((3, 3, 4)),
            dma((3, 3)),
            dma((3,)),
        ],
        compiler_params=pltpu.CompilerParams(
            collective_id=0, has_side_effects=True, vmem_limit_bytes=50 * 2**20
        ),
        cost_estimate=pl.CostEstimate(flops=4 * 2 * 512 * 512 * 8192, bytes_accessed=3 * 2**23, transcendentals=2**20),
        name="head_step",
    )(
        hidden, ref_hidden, w_policy, w_ref.reshape(4, 4, R, 8 * WIDTH),
        token_ids.reshape(1, T), loss_mask.reshape(1, T), advantages.reshape(1, T),
    )


def solution(mesh):
    placed = (
        P("section", "tensor"),
        P("section", "tensor"),
        P(("section", "tensor"), None),
        P(("section", "tensor"), None),
        P(),
        P(),
        P(),
    )
    return jax.shard_map(
        shards,
        mesh=mesh,
        in_specs=placed,
        out_specs=(P("section", "tensor"), P(("section", "tensor"), None)),
        check_vma=False,
    )
```
